512 devices in a mesh: ctx: 128 (over z, y_lo, x), ch: 4 (over y_hi, core).
Axes of the slice: x: 4, y: 4 (y_hi: 2, y_lo: 2; y = y_hi * 2 + y_lo), z: 16, core: 2. Of those that a mesh axis runs over, the one named last changes fastest.
Arguments:
- tokens: bfloat16 [16384, 4096], P('ctx'), may hold values from -1000 to 1000, as said below
- norm_gain: float32 [4096], replicated, may hold values from 0.1 to 1.9
- in_proj: bfloat16 [4096, 3, 2048], P('ctx', None, 'ch'), may hold values from -0.09375 to 0.09375
- short_taps: float32 [3, 3, 2048], P(None, None, 'ch'), may hold values from -3 to 3
- decay: float32 [16, 2048], P(None, 'ch'), may hold values from 0 to 1, as said below
- residue: float32 [16, 2048], P(None, 'ch'), may hold values from -1.5 to 1.5
- skip: float32 [2048], P('ch'), may hold values from -4 to 4
Outputs:
- mixed: bfloat16 [16384, 2048], P('ctx', 'ch')
The draws below stay inside these ranges and needn't reach their ends.
Inputs may be any that keep to these rules, and one draw needn't show every extreme that they name: `tokens`: every entry is finite. `decay`: every rate is positive.
All inputs are finite; a program needn't handle non-finite values.
Results may differ from the reference program's by a relative error of at most 0.01295.
Values may be sent and summed in bfloat16 or wider, within the bound.
A program may use at most 128 MiB of HBM per device.

```python
import math
import jax
import jax.numpy as jnp
from jax import lax

D = 4096
SLAB = 2048
TAPS = 3
MODES = 16
TOK_DEV = 128
SEQ = 16384


def draw_tokens(key, part):
    base_key, row_key, col_key = jax.random.split(key, 3)
    base = jax.random.normal(base_key, (SEQ, D), jnp.float32)
    base = jnp.clip(base, -6.0, 6.0)
    reach = math.log(10.0)
    row_scale = jnp.exp(jax.random.uniform(row_key, (SEQ, 1), jnp.float32, 0.0, reach))
    col_scale = jnp.exp(jax.random.uniform(col_key, (1, D), jnp.float32, 0.0, reach))
    return (base * row_scale * col_scale).astype(jnp.bfloat16)


def draw_decay(key, part):
    pick_key, slow_key, fast_key = jax.random.split(key, 3)
    share = 0.5
    chooser = jax.random.uniform(pick_key, (MODES, SLAB), jnp.float32)
    slow_rate = jnp.exp(jax.random.uniform(slow_key, (MODES, SLAB), jnp.float32, math.log(0.3 / SEQ), math.log(2.3 / SEQ)))
    fast_rate = jnp.exp(jax.random.uniform(fast_key, (MODES, SLAB), jnp.float32, math.log(1.0 / 50.0), math.log(1.0 / 20.0)))
    return jnp.where(chooser < share, slow_rate, fast_rate).astype(jnp.float32)


def shard_levels(key, extent, cuts, low, largest):
    def one(position, blocks):
        draws = jax.random.uniform(jax.random.fold_in(jax.random.fold_in(key, 6), position), (blocks,), jnp.float32, low / len(cuts), largest / len(cuts))
        return jnp.repeat(jnp.exp(draws), extent[position] // blocks).reshape((-1,) + (1,) * (len(extent) - position - 1))

    loudness = one(*cuts[0])
    for cut in cuts[1:]:
        loudness = loudness * one(*cut)
    return loudness


def scatter_about(own_key, extent, scale, most, cuts=(), held_as=jnp.bfloat16):
    array = scale * jax.random.normal(own_key, extent, jnp.float32)
    if cuts:
        array = array * shard_levels(own_key, extent, cuts, -0.22, 0.18)
    return jnp.clip(array, -most, most).astype(held_as)


def setup_inputs(seed: int = 0) -> dict:
    arg_keys = jax.random.split(jax.random.key(seed), 8)
    return {
        "tokens": draw_tokens(jax.random.fold_in(arg_keys[7], 71), 0),
        "norm_gain": jnp.clip(1.0 + 0.18 * jax.random.normal(arg_keys[1], (D,), jnp.float32), 0.1, 1.9),
        "in_proj": scatter_about(arg_keys[2], (D, 3, SLAB), D ** -0.5, 0.09375, ((0, 128), (2, 4))),
        "short_taps": scatter_about(arg_keys[3], (TAPS, 3, SLAB), 0.6, 3.0, ((2, 4),), jnp.float32),
        "decay": draw_decay(jax.random.fold_in(arg_keys[7], 71), 0),
        "residue": scatter_about(arg_keys[5], (MODES, SLAB), 0.25, 1.5, ((1, 4),), jnp.float32),
        "skip": scatter_about(arg_keys[6], (SLAB,), 1.0, 4.0, ((0, 4),), jnp.float32),
    }


def reference(tokens, norm_gain, in_proj, short_taps, decay, residue, skip):
    weights = in_proj.reshape(D, 3 * SLAB)

    def project(block_rows):
        as_float = block_rows.astype(jnp.float32)
        mean_square = lax.optimization_barrier(jnp.mean(as_float * as_float, axis=1, keepdims=True))
        normed = (as_float * lax.rsqrt(mean_square + 1e-06) * norm_gain).astype(jnp.bfloat16)
        return jnp.dot(normed, weights, preferred_element_type=jnp.float32).astype(jnp.bfloat16)
    blocked = tokens.reshape(SEQ // TOK_DEV, TOK_DEV, D)
    proj = lax.map(project, blocked).reshape(SEQ, 3, SLAB)
    padded = jnp.concatenate([jnp.zeros((TAPS - 1, 3, SLAB), jnp.bfloat16), proj], axis=0)
    feats = jnp.zeros((SEQ, 3, SLAB), jnp.float32)
    for shift_by in range(TAPS):
        window = padded[TAPS - 1 - shift_by:TAPS - 1 - shift_by + SEQ].astype(jnp.float32)
        feats = feats + short_taps[shift_by] * window
    drive = feats[:, 1, :] * feats[:, 2, :]
    positions = jnp.arange(SEQ).astype(jnp.float32)[:, None]
    filt = jnp.zeros((SEQ, SLAB), jnp.float32)
    for mode in range(MODES):
        amplitude = residue[mode] * jnp.sqrt(2.0 * decay[mode])
        filt = filt + amplitude * jnp.exp(-decay[mode] * positions)
    drive_spec = jnp.fft.fft(drive, n=2 * SEQ, axis=0)
    filt_spec = jnp.fft.fft(filt, n=2 * SEQ, axis=0)
    conv = jnp.real(jnp.fft.ifft(drive_spec * filt_spec, axis=0))[:SEQ].astype(jnp.float32)
    return (feats[:, 0, :] * (conv + skip * drive)).astype(jnp.bfloat16)
```

```python
import functools

import jax
import jax.numpy as jnp
from jax import lax
from jax.experimental import pallas as pl
from jax.experimental.pallas import tpu as pltpu
from jax.sharding import PartitionSpec as P

MESH = pl.DeviceIdType.MESH
F32 = jnp.float32
BF16 = jnp.bfloat16

ROWS = 128
GROUP = 8
PIECE = 16
LANES = 128
HALF = 64
MODES = 16


def kernel(
    nz,
    tok_ref,
    gain_ref,
    w_ref,
    taps_ref,
    dec_ref,
    res_ref,
    skip_ref,
    o_ref,
    X,
    wa,
    slabs,
    wfull,
    proj,
    rim,
    drive_s,
    gate_s,
    lam_s,
    amp_s,
    l64_s,
    step_s,
    pow_s,
    zw_s,
    end_s,
    totals,
    obuf,
    outbuf,
    inbox,
    wa_send,
    wa_recv,
    tok_send,
    tok_recv,
    sib_recv,
    zp_send,
    zp_recv,
    zm_send,
    zm_recv,
    rim_sem,
    st_send,
    st_recv,
    out_send,
    out_recv,
):
    ctx = lax.axis_index("ctx")
    ch = lax.axis_index("ch")
    z = ctx // 8
    q = ctx % 8
    y_lo = q // 4
    x = q % 4
    y_hi = ch // 2
    core = ch % 2
    par = q % 2
    tile = q // 2
    base = z * 8

    def plane(yl, xx):
        return yl * 4 + xx

    x_up = (base + plane(y_lo, (x + 1) % 4), ch)
    x_dn = (base + plane(y_lo, (x + 3) % 4), ch)
    y = y_hi * 2 + y_lo
    y_a = (y + 1) % 4
    y_b = (y + 3) % 4
    y_up = (base + plane(y_a % 2, x), (y_a // 2) * 2 + core)
    y_dn = (base + plane(y_b % 2, x), (y_b // 2) * 2 + core)
    sib = (ctx, y_hi * 2 + (1 - core))
    z_up = (((z + 1) % nz) * 8 + q, ch)
    z_dn = (((z + nz - 1) % nz) * 8 + q, ch)
    y_far = (base + plane(1 - y_lo, x), (1 - y_hi) * 2 + core)

    barrier = pltpu.get_barrier_semaphore()

    def greet(dev):
        pl.semaphore_signal(barrier, inc=1, device_id=dev, device_id_type=MESH)

    @pl.loop(1, GROUP)
    def _(d):
        greet((base + (q + d) % 8, ch))

    @pl.loop(1, nz)
    def _(d):
        greet((((z + d) % nz) * 8 + q, ch))

    greet(y_far)
    greet(sib)

    lane = lax.broadcasted_iota(jnp.int32, (8, LANES), 1)
    left = lane < HALF
    sub = lax.broadcasted_iota(jnp.int32, (8, LANES), 0)

    def swap(v):
        return pltpu.roll(v, HALF, 1)

    def pick(v, lf):
        r = swap(v)
        even = jnp.where(lf, v, r)
        odd = jnp.where(lf, r, v)
        return jnp.where(par == 0, even, odd)

    j_own = plane(y_lo, x)
    j_up = plane(y_lo, (x + 1) % 4)
    j_dn = plane(y_lo, (x + 3) % 4)
    j_op = plane(y_lo, (x + 2) % 4)
    p_own = plane(1 - y_lo, x)
    p_up = plane(1 - y_lo, (x + 1) % 4)
    p_dn = plane(1 - y_lo, (x + 3) % 4)
    p_op = plane(1 - y_lo, (x + 2) % 4)

    def norm(half, piece):
        rows = pl.ds(pl.multiple_of(half * HALF + piece * PIECE, PIECE), PIECE)
        v = tok_ref[rows, :].astype(F32)
        ms = jnp.mean(v * v, axis=1, keepdims=True)
        X[j_own, rows, :] = (v * lax.rsqrt(ms + 1e-06) * gain_ref[...]).astype(BF16)

    norm(core, 0)
    norm(core, 2)
    pl.semaphore_wait(barrier, 7 + (nz - 1) + 2)

    sent = []

    def wa_copy(d):
        to = (q + d) % 8
        lanes = pl.ds(pl.multiple_of((to // 2) * LANES, LANES), LANES)
        return pltpu.make_async_remote_copy(
            src_ref=w_ref.at[:, :, lanes],
            dst_ref=wa.at[q],
            send_sem=wa_send.at[d],
            recv_sem=wa_recv.at[d],
            device_id=(base + to, ch),
            device_id_type=MESH,
        )

    @pl.loop(1, GROUP)
    def _(d):
        wa_copy(d).start()

    count = [0]

    def piece_ref(j, half, piece):
        return X.at[j, pl.ds(pl.multiple_of(half * HALF + piece * PIECE, PIECE), PIECE), :]

    def send(j, piece, dev):
        ref = piece_ref(j, core, piece)
        recv = (sib_recv if dev is sib else tok_recv).at[j * 4 + piece]
        copy = pltpu.make_async_remote_copy(
            src_ref=ref,
            dst_ref=ref,
            send_sem=tok_send.at[count[0]],
            recv_sem=recv,
            device_id=dev,
            device_id_type=MESH,
        )
        count[0] += 1
        copy.start()
        sent.append(copy)

    def arrive(j, piece):
        ref = piece_ref(j, core, piece)
        pltpu.make_async_remote_copy(
            src_ref=ref,
            dst_ref=ref,
            send_sem=tok_send.at[0],
            recv_sem=tok_recv.at[j * 4 + piece],
            device_id=sib,
            device_id_type=MESH,
        ).wait_recv()

    def arrive_sib(j, piece):
        ref = piece_ref(j, 1 - core, piece)
        pltpu.make_async_remote_copy(
            src_ref=ref,
            dst_ref=ref,
            send_sem=tok_send.at[0],
            recv_sem=sib_recv.at[j * 4 + piece],
            device_id=sib,
            device_id_type=MESH,
        ).wait_recv()

    send(j_own, 0, x_up)
    send(j_own, 2, x_dn)
    send(j_own, 0, y_up)
    send(j_own, 2, y_dn)
    norm(core, 1)
    norm(core, 3)
    send(j_own, 1, x_up)
    send(j_own, 3, x_dn)
    send(j_own, 1, y_up)
    send(j_own, 3, y_dn)
    send(j_own, 2, x_up)
    send(j_own, 0, x_dn)
    send(j_own, 3, x_up)
    send(j_own, 1, x_dn)

    wa[q] = w_ref[:, :, pl.ds(pl.multiple_of(tile * LANES, LANES), LANES)]

    @pl.loop(1, GROUP)
    def _(d):
        copy = wa_copy(d)
        pltpu.make_async_remote_copy(
            src_ref=wa.at[(q + 8 - d) % 8],
            dst_ref=wa.at[(q + 8 - d) % 8],
            send_sem=wa_send.at[d],
            recv_sem=wa_recv.at[d],
            device_id=sib,
            device_id_type=MESH,
        ).wait_recv()
        copy.wait_send()

    lane32 = lax.broadcasted_iota(jnp.int32, (32, LANES), 1)
    left32 = lane32 < HALF
    for g in range(GROUP):
        qk = jnp.where(left32, pick(wa[g, 0].astype(F32), left32), pick(wa[g, 1].astype(F32), left32))
        slabs[z, g * 32 : (g + 1) * 32, :] = qk.astype(BF16)
    for g in range(GROUP // 2):
        v = jnp.where(
            left32, pick(wa[g, 2].astype(F32), left32), pick(wa[g + 4, 2].astype(F32), left32)
        )
        slabs[z, 256 + g * 32 : 256 + (g + 1) * 32, :] = v.astype(BF16)

    def z_copy(step, up):
        s = (z + nz - step) % nz if up else (z + step) % nz
        sems, recvs = (zp_send, zp_recv) if up else (zm_send, zm_recv)
        return pltpu.make_async_remote_copy(
            src_ref=slabs.at[s],
            dst_ref=slabs.at[s],
            send_sem=sems.at[step],
            recv_sem=recvs.at[step],
            device_id=z_up if up else z_dn,
            device_id_type=MESH,
        )

    def z_arrived(step, up):
        s = (z + 2 * nz - step - 1) % nz if up else (z + step + 1) % nz
        sems, recvs = (zp_send, zp_recv) if up else (zm_send, zm_recv)
        pltpu.make_async_remote_copy(
            src_ref=slabs.at[s],
            dst_ref=slabs.at[s],
            send_sem=sems.at[step],
            recv_sem=recvs.at[step],
            device_id=z_up if up else z_dn,
            device_id_type=MESH,
        ).wait_recv()
        return s

    def unpack(s):
        at = pl.multiple_of(s * 256, 256)
        wfull[pl.ds(at, 256), 0:LANES] = slabs[s, 0:256, :]
        v = slabs[s, 256:384, :]
        wfull[pl.ds(at, 128), LANES:] = v
        wfull[pl.ds(at + 128, 128), LANES:] = swap(v.astype(F32)).astype(BF16)

    n_up = nz // 2
    n_dn = nz - 1 - n_up

    def z_start(step):
        for up, most in ((True, n_up), (False, n_dn)):
            if step < most:
                copy = z_copy(step, up)
                copy.start()
                sent.append(copy)

    def z_round(step):
        got = []
        for up, most in ((True, n_up), (False, n_dn)):
            if step < most:
                got.append(z_arrived(step, up))
        z_start(step + 1)
        return got

    z_start(0)

    for piece in range(4):
        norm(1 - core, piece)
    unpack(z)

    lanes_q = pl.ds(pl.multiple_of(tile * LANES, LANES), LANES)
    lane16 = lax.broadcasted_iota(jnp.int32, (MODES, LANES), 1)
    left16 = lane16 < HALF
    dec = pick(dec_ref[:, lanes_q], left16)
    res = pick(res_ref[:, lanes_q], left16)
    skp = pick(skip_ref[:, lanes_q] * jnp.ones((8, LANES), F32), left)
    amp = res * jnp.sqrt(2.0 * dec)
    lam = jnp.exp(-dec)
    l64 = jnp.exp(-dec * 64.0)
    ones8 = jnp.ones((8, LANES), F32)
    subf = sub.astype(F32)

    def constants():
        for s in range(MODES):
            d8 = dec[s : s + 1, :] * ones8
            lam_s[s] = lam[s : s + 1, :] * ones8
            amp_s[s] = amp[s : s + 1, :] * ones8
            l64_s[s] = l64[s : s + 1, :] * ones8
            for i, sh in enumerate((1, 2, 4)):
                step_s[i, s] = jnp.where(sub >= sh, jnp.exp(-d8 * (128.0 * sh)), 0.0)
            pow_s[s] = jnp.exp(-d8 * (128.0 * subf))
        dec_p = jnp.where(left, dec[0:8, :], dec[8:16, :])
        for s in range(nz):
            gap = (z - 1 - s).astype(F32)
            zw_s[s] = jnp.where(s < z, jnp.exp(-dec_p * (1024.0 * jnp.maximum(gap, 0.0))), 0.0)

    rounds = [
        [(j_dn, 0, (x_up, y_up)), (j_up, 2, (x_dn, y_dn)), (p_own, 0, ()), (p_own, 2, ())],
        [(j_dn, 1, (x_up, y_up)), (j_up, 3, (x_dn, y_dn)), (p_own, 1, ()), (p_own, 3, ())],
        [(j_dn, 2, (y_dn,)), (j_up, 0, (y_up,)), (p_dn, 0, ()), (p_up, 2, ())],
        [(j_dn, 3, (y_dn,)), (j_up, 1, (y_up,)), (p_dn, 1, ()), (p_up, 3, ())],
        [(j_op, 0, (y_up,)), (j_op, 2, (y_dn,)), (p_up, 0, ()), (p_dn, 2, ())],
        [(j_op, 1, (y_up,)), (j_op, 3, (y_dn,)), (p_up, 1, ()), (p_dn, 3, ())],
        [(p_op, 0, ()), (p_op, 2, ())],
        [(p_op, 1, ()), (p_op, 3, ())],
    ]

    left64 = lax.broadcasted_iota(jnp.int32, (HALF, LANES), 1) < HALF

    def project(j):
        acc = jnp.dot(X[j], wfull[...], preferred_element_type=F32)
        t0a, t0b = acc[0:HALF, 0:LANES], acc[HALF:, 0:LANES]
        t1a, t1b = acc[0:HALF, LANES:], acc[HALF:, LANES:]
        rows = pl.ds(pl.multiple_of(j * HALF, HALF), HALF)
        for i, v in enumerate(
            (
                jnp.where(left64, t0a, swap(t0b)),
                jnp.where(left64, swap(t0a), t0b),
                jnp.where(left64, t1a, swap(t1b)),
            )
        ):
            proj[i, rows, :] = v.astype(BF16).astype(F32)

    def project_when_here(j):
        for piece in range(4):
            arrive_sib(j, piece)
        project(j)

    for r, events in enumerate(rounds):
        got = z_round(r) if r < 7 else []
        for j, piece, onward in events:
            arrive(j, piece)
            for dev in onward:
                send(j, piece, dev)
            send(j, piece, sib)
        for s in got:
            unpack(s)
        if r == 0:
            constants()
        if r == 6:
            for s in z_round(7):
                unpack(s)
            project(j_own)
            project_when_here(p_own)
            project_when_here(j_dn)
            project_when_here(j_up)
    project_when_here(j_op)
    project_when_here(p_up)
    project_when_here(p_dn)
    project_when_here(p_op)

    rim_copy = pltpu.make_async_remote_copy(
        src_ref=proj.at[:, 504:512, :],
        dst_ref=rim,
        send_sem=rim_sem.at[0],
        recv_sem=rim_sem.at[1],
        device_id=z_up,
        device_id_type=MESH,
    )
    rim_copy.start()
    rim_copy.wait_recv()

    def at_step(i, r):
        return proj[i, pl.ds(r, 8, stride=HALF), :]

    def before(i, back):
        last = swap(at_step(i, HALF - back))
        edge = swap(rim[i, 8 - back : 9 - back, :] * ones8)
        edge = jnp.where(z == 0, 0.0, edge)
        shifted = jnp.where(sub == 0, edge, pltpu.roll(last, 1, 0))
        return jnp.where(left, shifted, last)

    taps = [
        [pick(taps_ref[3 * k + i : 3 * k + i + 1, lanes_q] * ones8, left) for i in range(3)]
        for k in range(3)
    ]

    def scan_one(r, carry):
        one, two, states = carry
        now = [at_step(i, r) for i in range(3)]
        feats = [taps[0][i] * now[i] + taps[1][i] * one[i] + taps[2][i] * two[i] for i in range(3)]
        drive = feats[1] * feats[2]
        drive_s[r] = drive
        gate_s[r] = feats[0]
        states = [lam_s[s] * states[s] + drive for s in range(MODES)]
        return now, one, states

    start = (
        [before(i, 1) for i in range(3)],
        [before(i, 2) for i in range(3)],
        [jnp.zeros((8, LANES), F32)] * MODES,
    )
    ends = lax.fori_loop(0, HALF, scan_one, start)[2]

    for s in range(MODES):
        e = ends[s]
        sw = swap(e)
        el = jnp.where(left, e, sw)
        er = jnp.where(left, sw, e)
        g = l64_s[s] * el + er
        for i, sh in enumerate((1, 2, 4)):
            g = g + step_s[i, s] * pltpu.roll(g, sh, 0)
        end_s[0, s] = jnp.where(sub >= 1, pltpu.roll(g, 1, 0), 0.0)
        end_s[1, s] = el
        end_s[2, s] = g
    low = jnp.concatenate([end_s[2, s, 7:8, :] for s in range(8)], axis=0)
    high = jnp.concatenate([end_s[2, s, 7:8, :] for s in range(8, 16)], axis=0)
    totals[z] = jnp.where(left, low, high)

    def st_copy(d):
        return pltpu.make_async_remote_copy(
            src_ref=totals.at[z],
            dst_ref=totals.at[z],
            send_sem=st_send.at[d],
            recv_sem=st_recv.at[d],
            device_id=(((z + d) % nz) * 8 + q, ch),
            device_id_type=MESH,
        )

    @pl.loop(1, nz)
    def _(d):
        st_copy(d).start()

    @pl.loop(1, nz)
    def _(d):
        s = (z + nz - d) % nz
        pltpu.make_async_remote_copy(
            src_ref=totals.at[s],
            dst_ref=totals.at[s],
            send_sem=st_send.at[d],
            recv_sem=st_recv.at[d],
            device_id=sib,
            device_id_type=MESH,
        ).wait_recv()

    into = jnp.zeros((8, LANES), F32)
    for s in range(nz):
        into = into + zw_s[s] * totals[s]
    into_r = swap(into)
    into_lo = jnp.where(left, into, into_r)
    into_hi = jnp.where(left, into_r, into)

    states = []
    for s in range(MODES):
        zc = (into_lo if s < 8 else into_hi)[s % 8 : s % 8 + 1, :]
        c = end_s[0, s] + pow_s[s] * zc
        states.append(jnp.where(left, c, l64_s[s] * c + end_s[1, s]))

    def scan_two(r, states):
        drive = drive_s[r]
        states = [lam_s[s] * states[s] + drive for s in range(MODES)]
        terms = [amp_s[s] * states[s] for s in range(MODES)]
        while len(terms) > 1:
            terms = [a + b for a, b in zip(terms[::2], terms[1::2])]
        obuf[pl.ds(pl.multiple_of(r * 8, 8), 8), :] = gate_s[r] * (terms[0] + skp * drive)
        return states

    lax.fori_loop(0, HALF, scan_two, states)

    for j in range(GROUP):
        outbuf[j] = obuf[pl.ds(j, HALF, stride=8), :].astype(BF16)

    def out_copy(d):
        to = (q + d) % 8
        return pltpu.make_async_remote_copy(
            src_ref=outbuf.at[to],
            dst_ref=inbox.at[q],
            send_sem=out_send.at[d],
            recv_sem=out_recv.at[d],
            device_id=(base + to, ch),
            device_id_type=MESH,
        )

    @pl.loop(1, GROUP)
    def _(d):
        out_copy(d).start()

    inbox[q] = outbuf[q]

    for copy in sent:
        copy.wait_send()
    rim_copy.wait_send()

    @pl.loop(1, nz)
    def _(d):
        st_copy(d).wait_send()

    @pl.loop(1, GROUP)
    def _(d):
        out_copy(d).wait_send()
        g = (q + 8 - d) % 8
        pltpu.make_async_remote_copy(
            src_ref=inbox.at[g],
            dst_ref=inbox.at[g],
            send_sem=out_send.at[d],
            recv_sem=out_recv.at[d],
            device_id=sib,
            device_id_type=MESH,
        ).wait_recv()

    for g in range(GROUP // 2):
        a = inbox[2 * g].astype(F32)
        b = inbox[2 * g + 1].astype(F32)
        cols = slice(g * LANES, (g + 1) * LANES)
        o_ref[0:HALF, cols] = jnp.where(left64, a, swap(b)).astype(BF16)
        o_ref[HALF:, cols] = jnp.where(left64, swap(a), b).astype(BF16)


def local(tokens, norm_gain, in_proj, short_taps, decay, residue, skip):
    rows, width = tokens.shape
    channels = in_proj.shape[2]
    nz = lax.axis_size("ctx") // GROUP
    weights = jnp.transpose(in_proj, (1, 0, 2))
    vmem = pl.BlockSpec(memory_space=pltpu.VMEM)
    dma = pltpu.SemaphoreType.DMA
    const = pltpu.VMEM((MODES, 8, LANES), F32)
    return pl.pallas_call(
        functools.partial(kernel, nz),
        out_shape=jax.ShapeDtypeStruct((rows, channels), BF16),
        in_specs=[vmem] * 7,
        out_specs=vmem,
        scratch_shapes=[
            pltpu.VMEM((GROUP, ROWS, width), BF16),
            pltpu.VMEM((GROUP, 3, 32, LANES), BF16),
            pltpu.VMEM((nz, 384, LANES), BF16),
            pltpu.VMEM((width, 2 * LANES), BF16),
            pltpu.VMEM((3, GROUP * HALF, LANES), F32),
            pltpu.VMEM((3, 8, LANES), F32),
            pltpu.VMEM((HALF, 8, LANES), F32),
            pltpu.VMEM((HALF, 8, LANES), F32),
            const,
            const,
            const,
            pltpu.VMEM((3, MODES, 8, LANES), F32),
            const,
            pltpu.VMEM((nz, 8, LANES), F32),
            pltpu.VMEM((3, MODES, 8, LANES), F32),
            pltpu.VMEM((nz, 8, LANES), F32),
            pltpu.VMEM((GROUP * HALF, LANES), F32),
            pltpu.VMEM((GROUP, HALF, LANES), BF16),
            pltpu.VMEM((GROUP, HALF, LANES), BF16),
            dma((8,)),
            dma((8,)),
            dma((64,)),
            dma((32,)),
            dma((32,)),
            dma((8,)),
            dma((8,)),
            dma((8,)),
            dma((8,)),
            dma((2,)),
            dma((16,)),
            dma((16,)),
            dma((8,)),
            dma((8,)),
        ],
        compiler_params=pltpu.CompilerParams(
            collective_id=0, has_side_effects=True, vmem_limit_bytes=48 * 1024 * 1024
        ),
        name="hyena",
    )(
        tokens,
        norm_gain.reshape(1, width),
        weights,
        short_taps.reshape(9, channels),
        decay,
        residue,
        skip.reshape(1, channels),
    )


def solution(mesh):
    placed = (
        P("ctx", None),
        P(),
        P("ctx", None, "ch"),
        P(None, None, "ch"),
        P(None, "ch"),
        P(None, "ch"),
        P("ch"),
    )
    return jax.shard_map(
        local, mesh=mesh, in_specs=placed, out_specs=P("ctx", "ch"), check_vma=False
    )
```

```python
import functools

import jax
import jax.numpy as jnp
from jax import lax
from jax.experimental import pallas as pl
from jax.experimental.pallas import tpu as pltpu
from jax.sharding import PartitionSpec as P

MESH = pl.DeviceIdType.MESH
F32 = jnp.float32
BF16 = jnp.bfloat16

ROWS = 128
GROUP = 8
PIECE = 16
LANES = 128
HALF = 64
MODES = 16


def kernel(
    nz,
    tok_hbm,
    gain_hbm,
    w_hbm,
    taps_hbm,
    dec_hbm,
    res_hbm,
    skip_hbm,
    o_ref,
    tok_ref,
    gain_ref,
    taps_ref,
    dec_ref,
    res_ref,
    skip_ref,
    X,
    wa,
    slabs,
    wfull,
    part,
    proj,
    rim,
    drive_s,
    gate_s,
    lam_s,
    amp_s,
    l62_s,
    l64_s,
    step_s,
    pow_s,
    zw_s,
    end_s,
    totals,
    obuf,
    outbuf,
    inbox,
    in_sem,
    wa_send,
    wa_recv,
    tok_send,
    tok_recv,
    sib_recv,
    zp_send,
    zp_recv,
    zm_send,
    zm_recv,
    rim_sem,
    st_send,
    st_recv,
    out_send,
    out_recv,
):
    ctx = lax.axis_index("ctx")
    ch = lax.axis_index("ch")
    z = ctx // 8
    q = ctx % 8
    y_lo = q // 4
    x = q % 4
    y_hi = ch // 2
    core = ch % 2
    par = q % 2
    tile = q // 2
    base = z * 8

    def plane(yl, xx):
        return yl * 4 + xx

    x_up = (base + plane(y_lo, (x + 1) % 4), ch)
    x_dn = (base + plane(y_lo, (x + 3) % 4), ch)
    y = y_hi * 2 + y_lo
    y_a = (y + 1) % 4
    y_b = (y + 3) % 4
    y_up = (base + plane(y_a % 2, x), (y_a // 2) * 2 + core)
    y_dn = (base + plane(y_b % 2, x), (y_b // 2) * 2 + core)
    sib = (ctx, y_hi * 2 + (1 - core))
    z_up = (((z + 1) % nz) * 8 + q, ch)
    z_dn = (((z + nz - 1) % nz) * 8 + q, ch)
    y_far = (base + plane(1 - y_lo, x), (1 - y_hi) * 2 + core)

    def half_rows(half):
        return pl.ds(pl.multiple_of(half * HALF, HALF), HALF)

    fetch = [
        pltpu.make_async_copy(tok_hbm.at[half_rows(core), :], tok_ref.at[half_rows(core), :], in_sem.at[0]),
        pltpu.make_async_copy(gain_hbm, gain_ref, in_sem.at[1]),
        pltpu.make_async_copy(
            w_hbm.at[:, :, pl.ds(pl.multiple_of(tile * LANES, LANES), LANES)], wa.at[q], in_sem.at[2]
        ),
        pltpu.make_async_copy(
            tok_hbm.at[half_rows(1 - core), :], tok_ref.at[half_rows(1 - core), :], in_sem.at[3]
        ),
        pltpu.make_async_copy(dec_hbm, dec_ref, in_sem.at[4]),
        pltpu.make_async_copy(res_hbm, res_ref, in_sem.at[5]),
        pltpu.make_async_copy(taps_hbm, taps_ref, in_sem.at[6]),
        pltpu.make_async_copy(skip_hbm, skip_ref, in_sem.at[7]),
    ]
    for copy in fetch:
        copy.start()
    totals[...] = jnp.zeros_like(totals)

    barrier = pltpu.get_barrier_semaphore()

    def greet(dev):
        pl.semaphore_signal(barrier, inc=1, device_id=dev, device_id_type=MESH)

    @pl.loop(1, GROUP)
    def _(d):
        greet((base + (q + d) % 8, ch))

    @pl.loop(1, nz)
    def _(d):
        greet((((z + d) % nz) * 8 + q, ch))

    greet(y_far)
    greet(sib)

    lane = lax.broadcasted_iota(jnp.int32, (8, LANES), 1)
    left = lane < HALF
    sub = lax.broadcasted_iota(jnp.int32, (8, LANES), 0)

    def swap(v):
        return pltpu.roll(v, HALF, 1)

    def pick(v, lf):
        r = swap(v)
        even = jnp.where(lf, v, r)
        odd = jnp.where(lf, r, v)
        return jnp.where(par == 0, even, odd)

    j_own = plane(y_lo, x)
    j_up = plane(y_lo, (x + 1) % 4)
    j_dn = plane(y_lo, (x + 3) % 4)
    j_op = plane(y_lo, (x + 2) % 4)
    p_own = plane(1 - y_lo, x)
    p_up = plane(1 - y_lo, (x + 1) % 4)
    p_dn = plane(1 - y_lo, (x + 3) % 4)
    p_op = plane(1 - y_lo, (x + 2) % 4)

    def norm(half, piece):
        rows = pl.ds(pl.multiple_of(half * HALF + piece * PIECE, PIECE), PIECE)
        v = tok_ref[rows, :].astype(F32)
        ms = jnp.mean(v * v, axis=1, keepdims=True)
        X[j_own, rows, :] = (v * lax.rsqrt(ms + 1e-06) * gain_ref[...]).astype(BF16)

    fetch[0].wait()
    fetch[1].wait()
    norm(core, 0)
    norm(core, 2)
    pl.semaphore_wait(barrier, 7 + (nz - 1) + 2)

    sent = []

    def wa_copy(d):
        to = (q + d) % 8
        lanes = pl.ds(pl.multiple_of((to // 2) * LANES, LANES), LANES)
        return pltpu.make_async_remote_copy(
            src_ref=w_hbm.at[:, :, lanes],
            dst_ref=wa.at[q],
            send_sem=wa_send.at[d],
            recv_sem=wa_recv.at[d],
            device_id=(base + to, ch),
            device_id_type=MESH,
        )

    @pl.loop(1, GROUP)
    def _(d):
        wa_copy(d).start()

    count = [0]

    def piece_ref(j, half, piece):
        return X.at[j, pl.ds(pl.multiple_of(half * HALF + piece * PIECE, PIECE), PIECE), :]

    def send(j, piece, dev):
        ref = piece_ref(j, core, piece)
        recv = (sib_recv if dev is sib else tok_recv).at[j * 4 + piece]
        copy = pltpu.make_async_remote_copy(
            src_ref=ref,
            dst_ref=ref,
            send_sem=tok_send.at[count[0]],
            recv_sem=recv,
            device_id=dev,
            device_id_type=MESH,
        )
        count[0] += 1
        copy.start()
        sent.append(copy)

    def arrive(j, piece):
        ref = piece_ref(j, core, piece)
        pltpu.make_async_remote_copy(
            src_ref=ref,
            dst_ref=ref,
            send_sem=tok_send.at[0],
            recv_sem=tok_recv.at[j * 4 + piece],
            device_id=sib,
            device_id_type=MESH,
        ).wait_recv()

    def arrive_sib(j, piece):
        ref = piece_ref(j, 1 - core, piece)
        pltpu.make_async_remote_copy(
            src_ref=ref,
            dst_ref=ref,
            send_sem=tok_send.at[0],
            recv_sem=sib_recv.at[j * 4 + piece],
            device_id=sib,
            device_id_type=MESH,
        ).wait_recv()

    send(j_own, 0, x_up)
    send(j_own, 2, x_dn)
    send(j_own, 0, y_up)
    send(j_own, 2, y_dn)
    norm(core, 1)
    norm(core, 3)
    send(j_own, 1, x_up)
    send(j_own, 3, x_dn)
    send(j_own, 1, y_up)
    send(j_own, 3, y_dn)
    send(j_own, 2, x_up)
    send(j_own, 0, x_dn)
    send(j_own, 3, x_up)
    send(j_own, 1, x_dn)

    fetch[2].wait()

    @pl.loop(1, GROUP)
    def _(d):
        ref = wa.at[(q + 8 - d) % 8]
        pltpu.make_async_remote_copy(
            src_ref=ref,
            dst_ref=ref,
            send_sem=wa_send.at[d],
            recv_sem=wa_recv.at[d],
            device_id=sib,
            device_id_type=MESH,
        ).wait_recv()

    lane32 = lax.broadcasted_iota(jnp.int32, (32, LANES), 1)
    left32 = lane32 < HALF

    CHUNK = 128

    def z_ref(s, k):
        return slabs.at[s, pl.ds(k * CHUNK, CHUNK), :]

    def z_copy(step, up, k):
        s = (z + nz - step) % nz if up else (z + step) % nz
        sems, recvs = (zp_send, zp_recv) if up else (zm_send, zm_recv)
        return pltpu.make_async_remote_copy(
            src_ref=z_ref(s, k),
            dst_ref=z_ref(s, k),
            send_sem=sems.at[step * 3 + k],
            recv_sem=recvs.at[step * 3 + k],
            device_id=z_up if up else z_dn,
            device_id_type=MESH,
        )

    n_up = nz // 2
    n_dn = nz - 1 - n_up

    def z_send(step, up, k):
        if step < (n_up if up else n_dn):
            copy = z_copy(step, up, k)
            copy.start()
            sent.append(copy)

    def z_arrived(step, up, k):
        s = (z + 2 * nz - step - 1) % nz if up else (z + step + 1) % nz
        sems, recvs = (zp_send, zp_recv) if up else (zm_send, zm_recv)
        pltpu.make_async_remote_copy(
            src_ref=z_ref(s, k),
            dst_ref=z_ref(s, k),
            send_sem=sems.at[step * 3 + k],
            recv_sem=recvs.at[step * 3 + k],
            device_id=z_up if up else z_dn,
            device_id_type=MESH,
        ).wait_recv()
        return s

    def unpack(s):
        at = pl.multiple_of(s * 256, 256)
        wfull[pl.ds(at, 256), 0:LANES] = slabs[s, 0:256, :]
        v = slabs[s, 256:384, :]
        wfull[pl.ds(at, 128), LANES:] = v
        wfull[pl.ds(at + 128, 128), LANES:] = swap(v.astype(F32)).astype(BF16)

    for k in range(3):
        for g in range(4):
            if k < 2:
                n = k * 4 + g
                rows = jnp.where(left32, pick(wa[n, 0].astype(F32), left32), pick(wa[n, 1].astype(F32), left32))
            else:
                rows = jnp.where(
                    left32, pick(wa[g, 2].astype(F32), left32), pick(wa[g + 4, 2].astype(F32), left32)
                )
            slabs[z, k * CHUNK + g * 32 : k * CHUNK + (g + 1) * 32, :] = rows.astype(BF16)
        z_send(0, True, k)
        z_send(0, False, k)

    def z_round(step):
        got = []
        for k in range(3):
            for up, most in ((True, n_up), (False, n_dn)):
                if step < most:
                    s = z_arrived(step, up, k)
                    z_send(step + 1, up, k)
                    if k == 0:
                        got.append(s)
        return got

    for copy in fetch[3:]:
        copy.wait()
    lanes_q = pl.ds(pl.multiple_of(tile * LANES, LANES), LANES)
    lane16 = lax.broadcasted_iota(jnp.int32, (MODES, LANES), 1)
    left16 = lane16 < HALF
    ones8 = jnp.ones((8, LANES), F32)
    subf = sub.astype(F32)

    def constants(first):
        dec = pick(dec_ref[:, lanes_q], left16)
        amp = pick(res_ref[:, lanes_q], left16) * jnp.sqrt(2.0 * dec)
        for s in range(first, first + 4):
            d8 = dec[s : s + 1, :] * ones8
            amp_s[s] = amp[s : s + 1, :] * ones8
            lam_s[s] = jnp.exp(-d8)
            l62_s[s] = jnp.exp(-d8 * 62.0)
            l64_s[s] = jnp.exp(-d8 * 64.0)
            for i, sh in enumerate((1, 2, 4)):
                step_s[i, s] = jnp.where(sub >= sh, jnp.exp(-d8 * (128.0 * sh)), 0.0)
            pow_s[s] = jnp.exp(-d8 * (128.0 * subf))

    def z_weights():
        dec = pick(dec_ref[:, lanes_q], left16)
        dec_p = jnp.where(left, dec[0:8, :], dec[8:16, :])
        for s in range(nz):
            gap = (z - 1 - s).astype(F32)
            zw_s[s] = jnp.where(s < z, jnp.exp(-dec_p * (1024.0 * jnp.maximum(gap, 0.0))), 0.0)

    left64 = lax.broadcasted_iota(jnp.int32, (HALF, LANES), 1) < HALF

    def products(j, lo, hi):
        acc = None
        for d in range(lo, hi + 1):
            at = pl.multiple_of(((z + nz + d) % nz) * 256, 256)
            term = jnp.dot(X[j, :, pl.ds(at, 256)], wfull[pl.ds(at, 256), :], preferred_element_type=F32)
            acc = term if acc is None else acc + term
        return acc

    def here(j):
        if j is not j_own:
            for piece in range(4):
                arrive_sib(j, piece)

    def finish(j, acc):
        t0a, t0b = acc[0:HALF, 0:LANES], acc[HALF:, 0:LANES]
        t1a, t1b = acc[0:HALF, LANES:], acc[HALF:, LANES:]
        rows = half_rows(j)
        for i, v in enumerate(
            (
                jnp.where(left64, t0a, swap(t0b)),
                jnp.where(left64, swap(t0a), t0b),
                jnp.where(left64, t1a, swap(t1b)),
            )
        ):
            proj[i, rows, :] = v.astype(BF16).astype(F32)

    units = [
        [(j_dn, 0, (x_up, y_up)), (j_up, 2, (x_dn, y_dn)), (p_own, 0, ()), (p_own, 2, ())],
        [(j_dn, 1, (x_up, y_up)), (j_up, 3, (x_dn, y_dn)), (p_own, 1, ()), (p_own, 3, ())],
        [(j_dn, 2, (y_dn,)), (j_up, 0, (y_up,)), (p_dn, 0, ()), (p_up, 2, ())],
        [(j_dn, 3, (y_dn,)), (j_up, 1, (y_up,)), (p_dn, 1, (x_up,)), (p_up, 3, (x_dn,))],
        [(j_op, 0, (y_up,)), (j_op, 2, (y_dn,)), (p_up, 0, ()), (p_dn, 2, ())],
        [(j_op, 1, ()), (j_op, 3, ()), (p_up, 1, ()), (p_dn, 3, ())],
        [(p_op, 0, ()), (p_op, 2, ()), (p_op, 1, ()), (p_op, 3, ())],
    ]
    waiting = []

    def unit(u):
        for j, piece, onward in units[u]:
            arrive(j, piece)
            for dev in onward:
                send(j, piece, dev)
            waiting.append((j, piece))

    def to_sibling():
        for j, piece in waiting:
            send(j, piece, sib)
        waiting.clear()

    norm(1 - core, 0)
    norm(1 - core, 1)
    unpack(z)
    unit(0)
    for r in range(8):
        got = z_round(r)
        to_sibling()
        for s in got:
            unpack(s)
        if r == 0:
            norm(1 - core, 2)
            norm(1 - core, 3)
            unit(1)
        elif r == 1:
            constants(0)
            unit(2)
        elif r == 2:
            constants(4)
            constants(8)
        elif r == 3:
            constants(12)
            unit(3)
        elif r == 4:
            z_weights()
            unit(4)
        elif r == 5:
            for j in (j_own, p_own):
                here(j)
                part[j] = products(j, -6, 6)
            unit(5)
        elif r == 6:
            for j in (j_dn, j_up):
                here(j)
                part[j] = products(j, -7, 7)
            unit(6)
            to_sibling()
            for j in (j_op, p_up, p_dn):
                here(j)
                part[j] = products(j, -7, 7)
    for j in (j_own, p_own):
        finish(j, part[j] + products(j, -8, -7) + products(j, 7, 7))
    for j in (j_dn, j_up, j_op, p_up, p_dn):
        finish(j, part[j] + products(j, -8, -8))
    here(p_op)
    finish(p_op, products(p_op, -8, 7))

    rim_copy = pltpu.make_async_remote_copy(
        src_ref=proj.at[:, 504:512, :],
        dst_ref=rim,
        send_sem=rim_sem.at[0],
        recv_sem=rim_sem.at[1],
        device_id=z_up,
        device_id_type=MESH,
    )
    rim_copy.start()

    def at_step(i, r):
        return proj[i, pl.ds(r, 8, stride=HALF), :]

    def before(i, back, edge):
        last = swap(at_step(i, HALF - back))
        shifted = jnp.where(sub == 0, edge, pltpu.roll(last, 1, 0))
        return jnp.where(left, shifted, last)

    taps = [[pick(taps_ref[k, i : i + 1, lanes_q] * ones8, left) for i in range(3)] for k in range(3)]
    skp = pick(skip_ref[:, lanes_q] * ones8, left)

    def featurize(now, one, two):
        return [taps[0][i] * now[i] + taps[1][i] * one[i] + taps[2][i] * two[i] for i in range(3)]

    def scan_one(r, carry):
        one, two, states = carry
        now = [at_step(i, r) for i in range(3)]
        feats = featurize(now, one, two)
        drive = feats[1] * feats[2]
        drive_s[r] = drive
        gate_s[r] = feats[0]
        states = [lam_s[s] * states[s] + drive for s in range(MODES)]
        return now, one, states

    start = (
        [before(i, 1, 0.0) for i in range(3)],
        [before(i, 2, 0.0) for i in range(3)],
        [jnp.zeros((8, LANES), F32)] * MODES,
    )
    ends = lax.fori_loop(0, HALF, scan_one, start, unroll=2)[2]

    rim_copy.wait_recv()

    def edge(i, back):
        return jnp.where(z == 0, 0.0, swap(rim[i, 8 - back : 9 - back, :] * ones8))

    one = [before(i, 1, edge(i, 1)) for i in range(3)]
    two = [before(i, 2, edge(i, 2)) for i in range(3)]
    now = [at_step(i, 0) for i in range(3)]
    changes = []
    for r in range(2):
        feats = featurize(now, one, two)
        drive = feats[1] * feats[2]
        changes.append(drive - drive_s[r])
        drive_s[r] = drive
        gate_s[r] = feats[0]
        two, one, now = one, now, [at_step(i, 1) for i in range(3)]

    for s in range(MODES):
        e = ends[s] + l62_s[s] * (lam_s[s] * changes[0] + changes[1])
        sw = swap(e)
        el = jnp.where(left, e, sw)
        er = jnp.where(left, sw, e)
        g = l64_s[s] * el + er
        for i, sh in enumerate((1, 2, 4)):
            g = g + step_s[i, s] * pltpu.roll(g, sh, 0)
        end_s[0, s] = jnp.where(sub >= 1, pltpu.roll(g, 1, 0), 0.0)
        end_s[1, s] = el
        end_s[2, s] = g
    low = jnp.concatenate([end_s[2, s, 7:8, :] for s in range(8)], axis=0)
    high = jnp.concatenate([end_s[2, s, 7:8, :] for s in range(8, 16)], axis=0)
    totals[z] = jnp.where(left, low, high)

    def st_copy(d):
        return pltpu.make_async_remote_copy(
            src_ref=totals.at[z],
            dst_ref=totals.at[z],
            send_sem=st_send.at[d],
            recv_sem=st_recv.at[d],
            device_id=(((z + d) % nz) * 8 + q, ch),
            device_id_type=MESH,
        )

    far_first = sorted(range(1, nz), key=lambda d: -min(d, nz - d))
    for d in far_first:

        @pl.when(z + d < nz)
        def _(d=d):
            st_copy(d).start()

    for copy in sent:
        copy.wait_send()
    rim_copy.wait_send()

    @pl.loop(1, GROUP)
    def _(d):
        wa_copy(d).wait_send()

    for d in range(1, nz):

        @pl.when(z >= d)
        def _(d=d):
            s = (z + nz - d) % nz
            pltpu.make_async_remote_copy(
                src_ref=totals.at[s],
                dst_ref=totals.at[s],
                send_sem=st_send.at[d],
                recv_sem=st_recv.at[d],
                device_id=sib,
                device_id_type=MESH,
            ).wait_recv()

    into = jnp.zeros((8, LANES), F32)
    for s in range(nz):
        into = into + zw_s[s] * totals[s]
    into_r = swap(into)
    into_lo = jnp.where(left, into, into_r)
    into_hi = jnp.where(left, into_r, into)

    states = []
    for s in range(MODES):
        zc = (into_lo if s < 8 else into_hi)[s % 8 : s % 8 + 1, :]
        c = end_s[0, s] + pow_s[s] * zc
        states.append(jnp.where(left, c, l64_s[s] * c + end_s[1, s]))

    def scan_two(r, states):
        drive = drive_s[r]
        states = [lam_s[s] * states[s] + drive for s in range(MODES)]
        terms = [amp_s[s] * states[s] for s in range(MODES)]
        while len(terms) > 1:
            terms = [a + b for a, b in zip(terms[::2], terms[1::2])]
        obuf[pl.ds(pl.multiple_of(r * 8, 8), 8), :] = gate_s[r] * (terms[0] + skp * drive)
        return states

    lax.fori_loop(0, HALF, scan_two, states, unroll=2)

    for j in range(GROUP):
        outbuf[j] = obuf[pl.ds(j, HALF, stride=8), :].astype(BF16)

    def out_copy(d):
        to = (q + d) % 8
        return pltpu.make_async_remote_copy(
            src_ref=outbuf.at[to],
            dst_ref=inbox.at[q],
            send_sem=out_send.at[d],
            recv_sem=out_recv.at[d],
            device_id=(base + to, ch),
            device_id_type=MESH,
        )

    for d in (6, 2, 7, 5, 3, 1, 4):
        out_copy(d).start()

    inbox[q] = outbuf[q]

    for d in range(1, nz):

        @pl.when(z + d < nz)
        def _(d=d):
            st_copy(d).wait_send()

    @pl.loop(1, GROUP)
    def _(d):
        ref = inbox.at[(q + 8 - d) % 8]
        pltpu.make_async_remote_copy(
            src_ref=ref,
            dst_ref=ref,
            send_sem=out_send.at[d],
            recv_sem=out_recv.at[d],
            device_id=sib,
            device_id_type=MESH,
        ).wait_recv()
        out_copy(d).wait_send()

    for g in range(GROUP // 2):
        a = inbox[2 * g].astype(F32)
        b = inbox[2 * g + 1].astype(F32)
        cols = slice(g * LANES, (g + 1) * LANES)
        o_ref[0:HALF, cols] = jnp.where(left64, a, swap(b)).astype(BF16)
        o_ref[HALF:, cols] = jnp.where(left64, swap(a), b).astype(BF16)


def local(tokens, norm_gain, in_proj, short_taps, decay, residue, skip):
    rows, width = tokens.shape
    channels = in_proj.shape[2]
    nz = lax.axis_size("ctx") // GROUP
    weights = jnp.transpose(in_proj, (1, 0, 2))
    vmem = pl.BlockSpec(memory_space=pltpu.VMEM)
    dma = pltpu.SemaphoreType.DMA
    const = pltpu.VMEM((MODES, 8, LANES), F32)
    return pl.pallas_call(
        functools.partial(kernel, nz),
        out_shape=jax.ShapeDtypeStruct((rows, channels), BF16),
        in_specs=[pl.BlockSpec(memory_space=pl.ANY)] * 7,
        out_specs=vmem,
        scratch_shapes=[
            pltpu.VMEM((rows, width), BF16),
            pltpu.VMEM((1, width), F32),
            pltpu.VMEM((3, 3, channels), F32),
            pltpu.VMEM((MODES, channels), F32),
            pltpu.VMEM((MODES, channels), F32),
            pltpu.VMEM((1, channels), F32),
            pltpu.VMEM((GROUP, ROWS, width), BF16),
            pltpu.VMEM((GROUP, 3, 32, LANES), BF16),
            pltpu.VMEM((nz, 384, LANES), BF16),
            pltpu.VMEM((width, 2 * LANES), BF16),
            pltpu.VMEM((GROUP, ROWS, 2 * LANES), F32),
            pltpu.VMEM((3, GROUP * HALF, LANES), F32),
            pltpu.VMEM((3, 8, LANES), F32),
            pltpu.VMEM((HALF, 8, LANES), F32),
            pltpu.VMEM((HALF, 8, LANES), F32),
            const,
            const,
            const,
            const,
            pltpu.VMEM((3, MODES, 8, LANES), F32),
            const,
            pltpu.VMEM((nz, 8, LANES), F32),
            pltpu.VMEM((3, MODES, 8, LANES), F32),
            pltpu.VMEM((nz, 8, LANES), F32),
            pltpu.VMEM((GROUP * HALF, LANES), F32),
            pltpu.VMEM((GROUP, HALF, LANES), BF16),
            pltpu.VMEM((GROUP, HALF, LANES), BF16),
            dma((8,)),
            dma((8,)),
            dma((8,)),
            dma((64,)),
            dma((32,)),
            dma((32,)),
            dma((24,)),
            dma((24,)),
            dma((24,)),
            dma((24,)),
            dma((2,)),
            dma((16,)),
            dma((16,)),
            dma((8,)),
            dma((8,)),
        ],
        compiler_params=pltpu.CompilerParams(
            collective_id=0, has_side_effects=True, vmem_limit_bytes=56 * 1024 * 1024
        ),
        name="hyena",
    )(
        tokens,
        norm_gain.reshape(1, width),
        weights,
        short_taps,
        decay,
        residue,
        skip.reshape(1, channels),
    )


def solution(mesh):
    placed = (
        P("ctx", None),
        P(),
        P("ctx", None, "ch"),
        P(None, None, "ch"),
        P(None, "ch"),
        P(None, "ch"),
        P("ch"),
    )
    return jax.shard_map(
        local, mesh=mesh, in_specs=placed, out_specs=P("ctx", "ch"), check_vma=False
    )
```

```python
import functools

import jax
import jax.numpy as jnp
from jax import lax
from jax.experimental import pallas as pl
from jax.experimental.pallas import tpu as pltpu
from jax.sharding import PartitionSpec as P

MESH = pl.DeviceIdType.MESH
F32 = jnp.float32
BF16 = jnp.bfloat16

ROWS = 128
GROUP = 8
PIECE = 16
LANES = 128
HALF = 64
MODES = 16


def kernel(
    nz,
    tok_hbm,
    gain_hbm,
    w_hbm,
    taps_hbm,
    dec_hbm,
    res_hbm,
    skip_hbm,
    o_ref,
    tok_ref,
    gain_ref,
    w_ref,
    taps_ref,
    dec_ref,
    res_ref,
    skip_ref,
    X,
    wa,
    slabs,
    wfull,
    part,
    proj,
    rim,
    drive_s,
    gate_s,
    lam_s,
    amp_s,
    l62_s,
    l64_s,
    step_s,
    pow_s,
    zw_s,
    end_s,
    totals,
    obuf,
    outbuf,
    inbox,
    in_sem,
    wa_send,
    wa_recv,
    tok_send,
    tok_recv,
    sib_recv,
    zp_send,
    zp_recv,
    zm_send,
    zm_recv,
    sl_send,
    sl_recv,
    rim_sem,
    st_send,
    st_recv,
    out_send,
    out_recv,
):
    ctx = lax.axis_index("ctx")
    ch = lax.axis_index("ch")
    z = ctx // 8
    q = ctx % 8
    y_lo = q // 4
    x = q % 4
    y_hi = ch // 2
    core = ch % 2
    par = q % 2
    tile = q // 2
    base = z * 8

    def plane(yl, xx):
        return yl * 4 + xx

    x_up = (base + plane(y_lo, (x + 1) % 4), ch)
    x_dn = (base + plane(y_lo, (x + 3) % 4), ch)
    y = y_hi * 2 + y_lo
    y_a = (y + 1) % 4
    y_b = (y + 3) % 4
    y_up = (base + plane(y_a % 2, x), (y_a // 2) * 2 + core)
    y_dn = (base + plane(y_b % 2, x), (y_b // 2) * 2 + core)
    sib = (ctx, y_hi * 2 + (1 - core))
    z_up = (((z + 1) % nz) * 8 + q, ch)
    z_dn = (((z + nz - 1) % nz) * 8 + q, ch)
    y_far = (base + plane(1 - y_lo, x), (1 - y_hi) * 2 + core)

    def half_rows(half):
        return pl.ds(pl.multiple_of(half * HALF, HALF), HALF)

    pairs = (
        (tok_hbm.at[half_rows(core), :], tok_ref.at[half_rows(core), :]),
        (gain_hbm, gain_ref),
        (w_hbm, w_ref),
        (tok_hbm.at[half_rows(1 - core), :], tok_ref.at[half_rows(1 - core), :]),
        (dec_hbm, dec_ref),
        (res_hbm, res_ref),
        (taps_hbm, taps_ref),
        (skip_hbm, skip_ref),
    )
    fetch = [pltpu.make_async_copy(a, b, in_sem.at[i]) for i, (a, b) in enumerate(pairs)]
    for copy in fetch:
        copy.start()

    def w_lanes(chip):
        return pl.ds(pl.multiple_of((chip // 2) * LANES, LANES), LANES)

    totals[...] = jnp.zeros_like(totals)

    barrier = pltpu.get_barrier_semaphore()

    def greet(dev):
        pl.semaphore_signal(barrier, inc=1, device_id=dev, device_id_type=MESH)

    @pl.loop(1, GROUP)
    def _(d):
        greet((base + (q + d) % 8, ch))
        greet((base + (q + d) % 8, y_hi * 2 + (1 - core)))

    @pl.loop(1, nz)
    def _(d):
        greet((((z + d) % nz) * 8 + q, ch))

    greet(y_far)
    greet(sib)

    lane = lax.broadcasted_iota(jnp.int32, (8, LANES), 1)
    left = lane < HALF
    sub = lax.broadcasted_iota(jnp.int32, (8, LANES), 0)

    def swap(v):
        return pltpu.roll(v, HALF, 1)

    def pick(v, lf):
        r = swap(v)
        even = jnp.where(lf, v, r)
        odd = jnp.where(lf, r, v)
        return jnp.where(par == 0, even, odd)

    j_own = plane(y_lo, x)
    j_up = plane(y_lo, (x + 1) % 4)
    j_dn = plane(y_lo, (x + 3) % 4)
    j_op = plane(y_lo, (x + 2) % 4)
    p_own = plane(1 - y_lo, x)
    p_up = plane(1 - y_lo, (x + 1) % 4)
    p_dn = plane(1 - y_lo, (x + 3) % 4)
    p_op = plane(1 - y_lo, (x + 2) % 4)

    def norm(half, piece):
        rows = pl.ds(pl.multiple_of(half * HALF + piece * PIECE, PIECE), PIECE)
        v = tok_ref[rows, :].astype(F32)
        ms = jnp.mean(v * v, axis=1, keepdims=True)
        X[j_own, rows, :] = (v * lax.rsqrt(ms + 1e-06) * gain_ref[...]).astype(BF16)

    fetch[0].wait()
    fetch[1].wait()
    norm(core, 0)
    norm(core, 2)
    fetch[2].wait()
    pl.semaphore_wait(barrier, 7 + 7 + (nz - 1) + 2)

    sent = []

    def wa_copy(d):
        to = (q + d) % 8
        return pltpu.make_async_remote_copy(
            src_ref=w_ref.at[:, :, w_lanes(to)],
            dst_ref=wa.at[core, q],
            send_sem=wa_send.at[d],
            recv_sem=wa_recv.at[core * 8 + d],
            device_id=(base + to, y_hi * 2 + 1),
            device_id_type=MESH,
        )

    @pl.loop(1, GROUP)
    def _(d):
        wa_copy(d).start()

    @pl.when(core == 0)
    def _():
        wa_copy(0).start()

    count = [0]

    def piece_ref(j, half, piece):
        return X.at[j, pl.ds(pl.multiple_of(half * HALF + piece * PIECE, PIECE), PIECE), :]

    def send(j, piece, dev):
        ref = piece_ref(j, core, piece)
        recv = (sib_recv if dev is sib else tok_recv).at[j * 4 + piece]
        copy = pltpu.make_async_remote_copy(
            src_ref=ref,
            dst_ref=ref,
            send_sem=tok_send.at[count[0]],
            recv_sem=recv,
            device_id=dev,
            device_id_type=MESH,
        )
        count[0] += 1
        sent.append(copy)
        return copy

    def arrive(j, piece):
        ref = piece_ref(j, core, piece)
        pltpu.make_async_remote_copy(
            src_ref=ref,
            dst_ref=ref,
            send_sem=tok_send.at[0],
            recv_sem=tok_recv.at[j * 4 + piece],
            device_id=sib,
            device_id_type=MESH,
        ).wait_recv()

    def arrive_sib(j, piece):
        ref = piece_ref(j, 1 - core, piece)
        pltpu.make_async_remote_copy(
            src_ref=ref,
            dst_ref=ref,
            send_sem=tok_send.at[0],
            recv_sem=sib_recv.at[j * 4 + piece],
            device_id=sib,
            device_id_type=MESH,
        ).wait_recv()

    send(j_own, 0, x_up).start()
    send(j_own, 2, x_dn).start()
    send(j_own, 0, y_up).start()
    send(j_own, 2, y_dn).start()
    norm(core, 1)
    norm(core, 3)
    send(j_own, 1, x_up).start()
    send(j_own, 3, x_dn).start()
    send(j_own, 1, y_up).start()
    send(j_own, 3, y_dn).start()
    send(j_own, 2, x_up).start()
    send(j_own, 0, x_dn).start()
    send(j_own, 3, x_up).start()
    send(j_own, 1, x_dn).start()

    lane32 = lax.broadcasted_iota(jnp.int32, (32, LANES), 1)
    left32 = lane32 < HALF

    CHUNK = 128
    last = nz // 2 - 1
    ways = (True, False)
    turns = [(c, k, up) for c in (1, 0) for k in range(3) for up in ways]

    def goes(step, up, c):
        return step < last or (step == last and c == (0 if up else 1))

    def z_copy(s, step, up, c, k):
        sems, recvs = (zp_send, zp_recv) if up else (zm_send, zm_recv)
        ref = slabs.at[c, s, pl.ds(k * CHUNK, CHUNK), :]
        return pltpu.make_async_remote_copy(
            src_ref=ref,
            dst_ref=ref,
            send_sem=sems.at[step * 6 + c * 3 + k],
            recv_sem=recvs.at[step * 6 + c * 3 + k],
            device_id=z_up if up else z_dn,
            device_id_type=MESH,
        )

    def z_out(step, up, c, k):
        return z_copy((z + nz - step) % nz if up else (z + step) % nz, step, up, c, k)

    def z_in(step, up, c, k):
        return z_copy(z_slab(step, up), step, up, c, k)

    def z_slab(step, up):
        return (z + 2 * nz - step - 1) % nz if up else (z + step + 1) % nz

    def hand_over(s, n):
        ref = slabs.at[0, s]
        return pltpu.make_async_remote_copy(
            src_ref=ref,
            dst_ref=ref,
            send_sem=sl_send.at[n],
            recv_sem=sl_recv.at[n],
            device_id=sib,
            device_id_type=MESH,
        )

    def came(step):
        if step < 0:
            return [(z, 15)]
        if step == last:
            return [(z_slab(step, True), step * 2)]
        return [(z_slab(step, up), step * 2 + (0 if up else 1)) for up in ways]

    @pl.when(core == 1)
    def _():
        wa[1, q] = w_ref[:, :, w_lanes(q)]
        for c in (1, 0):
            for d in range(c, GROUP):
                ref = wa.at[c, (q + 8 - d) % 8]
                pltpu.make_async_remote_copy(
                    src_ref=ref,
                    dst_ref=ref,
                    send_sem=wa_send.at[d],
                    recv_sem=wa_recv.at[c * 8 + d],
                    device_id=sib,
                    device_id_type=MESH,
                ).wait_recv()
            for k in range(3):
                for g in range(4):
                    if k < 2:
                        lo, hi = wa[c, k * 4 + g, 0], wa[c, k * 4 + g, 1]
                    else:
                        lo, hi = wa[c, g, 2], wa[c, g + 4, 2]
                    rows = jnp.where(left32, pick(lo.astype(F32), left32), pick(hi.astype(F32), left32))
                    slabs[c, z, k * CHUNK + g * 32 : k * CHUNK + (g + 1) * 32, :] = rows.astype(BF16)
                z_out(0, True, c, k).start()
                z_out(0, False, c, k).start()
        hand_over(z, 15).start()

    def unpack(s, n):
        @pl.when(core == 0)
        def _():
            hand_over(s, n).wait_recv()

        at = pl.multiple_of(s * 256, 256)
        wfull[pl.ds(at, 256), 0:LANES] = slabs[core, s, 0:256, :]
        v = slabs[core, s, 256:384, :]
        wfull[pl.ds(at, 128), LANES:] = v
        wfull[pl.ds(at + 128, 128), LANES:] = swap(v.astype(F32)).astype(BF16)

    def unpacks(step):
        return [functools.partial(unpack, s, n) for s, n in came(step)]

    def z_round(step, tasks):
        @pl.when(core == 1)
        def _():
            todo = list(tasks)
            for c, k, up in turns:
                if goes(step, up, c):
                    z_in(step, up, c, k).wait_recv()
                if goes(step + 1, up, c):
                    z_out(step + 1, up, c, k).start()
                if (c, k, up) == turns[-1]:
                    for s, n in came(step):
                        hand_over(s, n).start()
                if todo:
                    todo.pop(0)()
            for task in todo:
                task()

        @pl.when(core == 0)
        def _():
            for task in tasks:
                task()

    for copy in fetch[3:]:
        copy.wait()
    lanes_q = pl.ds(pl.multiple_of(tile * LANES, LANES), LANES)
    lane16 = lax.broadcasted_iota(jnp.int32, (MODES, LANES), 1)
    left16 = lane16 < HALF
    ones8 = jnp.ones((8, LANES), F32)
    subf = sub.astype(F32)

    def constants(first):
        dec = pick(dec_ref[:, lanes_q], left16)
        amp = pick(res_ref[:, lanes_q], left16) * jnp.sqrt(2.0 * dec)
        for s in (first, first + 1):
            d8 = dec[s : s + 1, :] * ones8
            amp_s[s] = amp[s : s + 1, :] * ones8
            lam_s[s] = jnp.exp(-d8)
            l62_s[s] = jnp.exp(-d8 * 62.0)
            l64_s[s] = jnp.exp(-d8 * 64.0)
            for i, sh in enumerate((1, 2, 4)):
                step_s[i, s] = jnp.where(sub >= sh, jnp.exp(-d8 * (128.0 * sh)), 0.0)
            pow_s[s] = jnp.exp(-d8 * (128.0 * subf))

    def z_weights():
        dec = pick(dec_ref[:, lanes_q], left16)
        dec_p = jnp.where(left, dec[0:8, :], dec[8:16, :])
        for s in range(nz):
            gap = (z - 1 - s).astype(F32)
            zw_s[s] = jnp.where(s < z, jnp.exp(-dec_p * (1024.0 * jnp.maximum(gap, 0.0))), 0.0)

    left64 = lax.broadcasted_iota(jnp.int32, (HALF, LANES), 1) < HALF

    def products(j, steps):
        acc = None
        for d in steps:
            at = pl.multiple_of(((z + nz + d) % nz) * 256, 256)
            term = jnp.dot(X[j, :, pl.ds(at, 256)], wfull[pl.ds(at, 256), :], preferred_element_type=F32)
            acc = term if acc is None else acc + term
        return acc

    def here(j):
        for piece in range(4):
            arrive_sib(j, piece)

    def add_products(j, steps, first):
        if first and j is not j_own:
            here(j)
        acc = products(j, steps)
        part[j] = acc if first else part[j] + acc

    done = {}

    def product_tasks(j, reach, each=3):
        steps = sorted(range(-reach, reach + 1), key=abs)
        done[id(j)] = steps
        return [
            functools.partial(add_products, j, steps[i : i + each], i == 0) for i in range(0, len(steps), each)
        ]

    def finish(j, acc):
        t0a, t0b = acc[0:HALF, 0:LANES], acc[HALF:, 0:LANES]
        t1a, t1b = acc[0:HALF, LANES:], acc[HALF:, LANES:]
        rows = half_rows(j)
        for i, v in enumerate(
            (
                jnp.where(left64, t0a, swap(t0b)),
                jnp.where(left64, swap(t0a), t0b),
                jnp.where(left64, t1a, swap(t1b)),
            )
        ):
            proj[i, rows, :] = v.astype(BF16).astype(F32)

    units = [
        [(j_dn, 0, (x_up, y_up)), (j_up, 2, (x_dn, y_dn)), (p_own, 0, ()), (p_own, 2, ())],
        [(j_dn, 1, (x_up, y_up)), (j_up, 3, (x_dn, y_dn)), (p_own, 1, ()), (p_own, 3, ())],
        [(j_dn, 2, (y_dn,)), (j_up, 0, (y_up,)), (p_dn, 0, ()), (p_up, 2, ())],
        [(j_dn, 3, (y_dn,)), (j_up, 1, (y_up,)), (p_dn, 1, (x_up,)), (p_up, 3, (x_dn,))],
        [(j_op, 0, (y_up,)), (j_op, 2, (y_dn,)), (p_up, 0, ()), (p_dn, 2, ())],
        [(j_op, 1, ()), (j_op, 3, ()), (p_up, 1, ()), (p_dn, 3, ())],
        [(p_op, 0, ()), (p_op, 2, ()), (p_op, 1, ()), (p_op, 3, ())],
    ]
    waiting = []

    def unit(u):
        for j, piece, onward in units[u]:
            arrive(j, piece)
            for dev in onward:
                send(j, piece, dev).start()
            waiting.append((j, piece))

    def to_sibling():
        tasks = [send(j, piece, sib).start for j, piece in waiting]
        waiting.clear()
        return tasks

    def consts(*firsts):
        return [functools.partial(constants, s) for s in firsts]

    for piece in range(4):
        norm(1 - core, piece)
    unit(0)
    z_round(0, to_sibling() + unpacks(-1) + consts(0, 2))
    unit(1)
    z_round(1, to_sibling() + unpacks(0) + consts(4, 6, 8))
    unit(2)
    z_round(2, to_sibling() + unpacks(1) + consts(10, 12, 14))
    z_round(3, unpacks(2) + [z_weights])
    unit(3)
    z_round(4, to_sibling() + unpacks(3) + product_tasks(j_own, 4))
    unit(4)
    z_round(5, to_sibling() + unpacks(4) + product_tasks(p_own, 5))
    unit(5)
    z_round(6, to_sibling() + unpacks(5) + product_tasks(j_dn, 6) + product_tasks(j_up, 6))
    unit(6)
    for task in to_sibling():
        task()
    z_round(
        7,
        unpacks(6)
        + product_tasks(j_op, 7)
        + product_tasks(p_up, 7)
        + product_tasks(p_dn, 7)
        + product_tasks(p_op, 7),
    )
    for task in unpacks(7):
        task()
    for j in (j_own, p_own, j_dn, j_up, j_op, p_up, p_dn, p_op):
        finish(j, part[j] + products(j, [d for d in range(-8, 8) if d not in done[id(j)]]))

    rim_copy = pltpu.make_async_remote_copy(
        src_ref=proj.at[:, 504:512, :],
        dst_ref=rim,
        send_sem=rim_sem.at[0],
        recv_sem=rim_sem.at[1],
        device_id=z_up,
        device_id_type=MESH,
    )
    rim_copy.start()

    def at_step(i, r):
        return proj[i, pl.ds(r, 8, stride=HALF), :]

    def before(i, back, edge):
        last = swap(at_step(i, HALF - back))
        shifted = jnp.where(sub == 0, edge, pltpu.roll(last, 1, 0))
        return jnp.where(left, shifted, last)

    taps = [[pick(taps_ref[k, i : i + 1, lanes_q] * ones8, left) for i in range(3)] for k in range(3)]
    skp = pick(skip_ref[:, lanes_q] * ones8, left)

    def featurize(now, one, two):
        return [taps[0][i] * now[i] + taps[1][i] * one[i] + taps[2][i] * two[i] for i in range(3)]

    def scan_one(r, carry):
        one, two, states = carry
        now = [at_step(i, r) for i in range(3)]
        feats = featurize(now, one, two)
        drive = feats[1] * feats[2]
        drive_s[r] = drive
        gate_s[r] = feats[0]
        states = [lam_s[s] * states[s] + drive for s in range(MODES)]
        return now, one, states

    start = (
        [before(i, 1, 0.0) for i in range(3)],
        [before(i, 2, 0.0) for i in range(3)],
        [jnp.zeros((8, LANES), F32)] * MODES,
    )
    ends = lax.fori_loop(0, HALF, scan_one, start, unroll=2)[2]

    rim_copy.wait_recv()

    def edge(i, back):
        return jnp.where(z == 0, 0.0, swap(rim[i, 8 - back : 9 - back, :] * ones8))

    one = [before(i, 1, edge(i, 1)) for i in range(3)]
    two = [before(i, 2, edge(i, 2)) for i in range(3)]
    now = [at_step(i, 0) for i in range(3)]
    changes = []
    for r in range(2):
        feats = featurize(now, one, two)
        drive = feats[1] * feats[2]
        changes.append(drive - drive_s[r])
        drive_s[r] = drive
        gate_s[r] = feats[0]
        two, one, now = one, now, [at_step(i, 1) for i in range(3)]

    for s in range(MODES):
        e = ends[s] + l62_s[s] * (lam_s[s] * changes[0] + changes[1])
        sw = swap(e)
        el = jnp.where(left, e, sw)
        er = jnp.where(left, sw, e)
        g = l64_s[s] * el + er
        for i, sh in enumerate((1, 2, 4)):
            g = g + step_s[i, s] * pltpu.roll(g, sh, 0)
        end_s[0, s] = jnp.where(sub >= 1, pltpu.roll(g, 1, 0), 0.0)
        end_s[1, s] = el
        end_s[2, s] = g
    low = jnp.concatenate([end_s[2, s, 7:8, :] for s in range(8)], axis=0)
    high = jnp.concatenate([end_s[2, s, 7:8, :] for s in range(8, 16)], axis=0)
    totals[z] = jnp.where(left, low, high)

    def st_copy(d):
        return pltpu.make_async_remote_copy(
            src_ref=totals.at[z],
            dst_ref=totals.at[z],
            send_sem=st_send.at[d],
            recv_sem=st_recv.at[d],
            device_id=(((z + d) % nz) * 8 + q, ch),
            device_id_type=MESH,
        )

    far_first = sorted(range(1, nz), key=lambda d: -min(d, nz - d))
    for d in far_first:

        @pl.when(z + d < nz)
        def _(d=d):
            st_copy(d).start()

    for copy in sent:
        copy.wait_send()
    rim_copy.wait_send()

    @pl.loop(1, GROUP)
    def _(d):
        wa_copy(d).wait_send()

    @pl.when(core == 0)
    def _():
        wa_copy(0).wait_send()

    @pl.when(core == 1)
    def _():
        for step in range(last + 1):
            for c, k, up in turns:
                if goes(step, up, c):
                    z_out(step, up, c, k).wait_send()
        for step in range(-1, last + 1):
            for s, n in came(step):
                hand_over(s, n).wait_send()

    for d in range(1, nz):

        @pl.when(z >= d)
        def _(d=d):
            s = (z + nz - d) % nz
            pltpu.make_async_remote_copy(
                src_ref=totals.at[s],
                dst_ref=totals.at[s],
                send_sem=st_send.at[d],
                recv_sem=st_recv.at[d],
                device_id=sib,
                device_id_type=MESH,
            ).wait_recv()

    into = jnp.zeros((8, LANES), F32)
    for s in range(nz):
        into = into + zw_s[s] * totals[s]
    into_r = swap(into)
    into_lo = jnp.where(left, into, into_r)
    into_hi = jnp.where(left, into_r, into)

    states = []
    for s in range(MODES):
        zc = (into_lo if s < 8 else into_hi)[s % 8 : s % 8 + 1, :]
        c = end_s[0, s] + pow_s[s] * zc
        states.append(jnp.where(left, c, l64_s[s] * c + end_s[1, s]))

    def scan_two(r, states):
        drive = drive_s[r]
        states = [lam_s[s] * states[s] + drive for s in range(MODES)]
        terms = [amp_s[s] * states[s] for s in range(MODES)]
        while len(terms) > 1:
            terms = [a + b for a, b in zip(terms[::2], terms[1::2])]
        obuf[pl.ds(pl.multiple_of(r * 8, 8), 8), :] = gate_s[r] * (terms[0] + skp * drive)
        return states

    lax.fori_loop(0, HALF, scan_two, states, unroll=2)

    for j in range(GROUP):
        outbuf[j] = obuf[pl.ds(j, HALF, stride=8), :].astype(BF16)

    def out_copy(d):
        to = (q + d) % 8
        return pltpu.make_async_remote_copy(
            src_ref=outbuf.at[to],
            dst_ref=inbox.at[q],
            send_sem=out_send.at[d],
            recv_sem=out_recv.at[d],
            device_id=(base + to, ch),
            device_id_type=MESH,
        )

    for d in (6, 2, 7, 5, 3, 1, 4):
        out_copy(d).start()

    inbox[q] = outbuf[q]

    for d in range(1, nz):

        @pl.when(z + d < nz)
        def _(d=d):
            st_copy(d).wait_send()

    @pl.loop(1, GROUP)
    def _(d):
        ref = inbox.at[(q + 8 - d) % 8]
        pltpu.make_async_remote_copy(
            src_ref=ref,
            dst_ref=ref,
            send_sem=out_send.at[d],
            recv_sem=out_recv.at[d],
            device_id=sib,
            device_id_type=MESH,
        ).wait_recv()
        out_copy(d).wait_send()

    for g in range(GROUP // 2):
        a = inbox[2 * g].astype(F32)
        b = inbox[2 * g + 1].astype(F32)
        cols = slice(g * LANES, (g + 1) * LANES)
        o_ref[0:HALF, cols] = jnp.where(left64, a, swap(b)).astype(BF16)
        o_ref[HALF:, cols] = jnp.where(left64, swap(a), b).astype(BF16)


def local(tokens, norm_gain, in_proj, short_taps, decay, residue, skip):
    rows, width = tokens.shape
    channels = in_proj.shape[2]
    nz = lax.axis_size("ctx") // GROUP
    weights = jnp.transpose(in_proj, (1, 0, 2))
    vmem = pl.BlockSpec(memory_space=pltpu.VMEM)
    dma = pltpu.SemaphoreType.DMA
    const = pltpu.VMEM((MODES, 8, LANES), F32)
    return pl.pallas_call(
        functools.partial(kernel, nz),
        out_shape=jax.ShapeDtypeStruct((rows, channels), BF16),
        in_specs=[pl.BlockSpec(memory_space=pl.ANY)] * 7,
        out_specs=vmem,
        scratch_shapes=[
            pltpu.VMEM((rows, width), BF16),
            pltpu.VMEM((1, width), F32),
            pltpu.VMEM((3, 32, channels), BF16),
            pltpu.VMEM((3, 3, channels), F32),
            pltpu.VMEM((MODES, channels), F32),
            pltpu.VMEM((MODES, channels), F32),
            pltpu.VMEM((1, channels), F32),
            pltpu.VMEM((GROUP, ROWS, width), BF16),
            pltpu.VMEM((2, GROUP, 3, 32, LANES), BF16),
            pltpu.VMEM((2, nz, 384, LANES), BF16),
            pltpu.VMEM((width, 2 * LANES), BF16),
            pltpu.VMEM((GROUP, ROWS, 2 * LANES), F32),
            pltpu.VMEM((3, GROUP * HALF, LANES), F32),
            pltpu.VMEM((3, 8, LANES), F32),
            pltpu.VMEM((HALF, 8, LANES), F32),
            pltpu.VMEM((HALF, 8, LANES), F32),
            const,
            const,
            const,
            const,
            pltpu.VMEM((3, MODES, 8, LANES), F32),
            const,
            pltpu.VMEM((nz, 8, LANES), F32),
            pltpu.VMEM((3, MODES, 8, LANES), F32),
            pltpu.VMEM((nz, 8, LANES), F32),
            pltpu.VMEM((GROUP * HALF, LANES), F32),
            pltpu.VMEM((GROUP, HALF, LANES), BF16),
            pltpu.VMEM((GROUP, HALF, LANES), BF16),
            dma((8,)),
            dma((8,)),
            dma((16,)),
            dma((64,)),
            dma((32,)),
            dma((32,)),
            dma((48,)),
            dma((48,)),
            dma((48,)),
            dma((48,)),
            dma((16,)),
            dma((16,)),
            dma((2,)),
            dma((16,)),
            dma((16,)),
            dma((8,)),
            dma((8,)),
        ],
        compiler_params=pltpu.CompilerParams(
            collective_id=0, has_side_effects=True, vmem_limit_bytes=56 * 1024 * 1024
        ),
        name="hyena",
    )(
        tokens,
        norm_gain.reshape(1, width),
        weights,
        short_taps,
        decay,
        residue,
        skip.reshape(1, channels),
    )


def solution(mesh):
    placed = (
        P("ctx", None),
        P(),
        P("ctx", None, "ch"),
        P(None, None, "ch"),
        P(None, "ch"),
        P(None, "ch"),
        P("ch"),
    )
    return jax.shard_map(
        local, mesh=mesh, in_specs=placed, out_specs=P("ctx", "ch"), check_vma=False
    )
```

```python
import functools

import jax
import jax.numpy as jnp
from jax import lax
from jax.experimental import pallas as pl
from jax.experimental.pallas import tpu as pltpu
from jax.sharding import PartitionSpec as P

MESH = pl.DeviceIdType.MESH
F32 = jnp.float32
BF16 = jnp.bfloat16

ROWS = 128
GROUP = 8
PIECE = 16
LANES = 128
HALF = 64
MODES = 16


def kernel(
    nz,
    tok_hbm,
    gain_hbm,
    w_hbm,
    taps_hbm,
    dec_hbm,
    res_hbm,
    skip_hbm,
    o_ref,
    tok_ref,
    gain_ref,
    w_ref,
    taps_ref,
    dec_ref,
    res_ref,
    skip_ref,
    X,
    wpack,
    slabs,
    wfull,
    part,
    proj,
    rim,
    drive_s,
    gate_s,
    lam_s,
    amp_s,
    l62_s,
    l64_s,
    step_s,
    pow_s,
    zw_s,
    end_s,
    totals,
    obuf,
    outbuf,
    inbox,
    in_sem,
    wa_send,
    wa_recv,
    tok_send,
    tok_recv,
    sib_recv,
    zp_send,
    zp_recv,
    zm_send,
    zm_recv,
    sl_send,
    sl_recv,
    rim_sem,
    st_send,
    st_recv,
    out_send,
    out_recv,
):
    ctx = lax.axis_index("ctx")
    ch = lax.axis_index("ch")
    z = ctx // 8
    q = ctx % 8
    y_lo = q // 4
    x = q % 4
    y_hi = ch // 2
    core = ch % 2
    par = q % 2
    tile = q // 2
    base = z * 8

    def plane(yl, xx):
        return yl * 4 + xx

    x_up = (base + plane(y_lo, (x + 1) % 4), ch)
    x_dn = (base + plane(y_lo, (x + 3) % 4), ch)
    y = y_hi * 2 + y_lo
    y_a = (y + 1) % 4
    y_b = (y + 3) % 4
    y_up = (base + plane(y_a % 2, x), (y_a // 2) * 2 + core)
    y_dn = (base + plane(y_b % 2, x), (y_b // 2) * 2 + core)
    sib = (ctx, y_hi * 2 + (1 - core))
    z_up = (((z + 1) % nz) * 8 + q, ch)
    z_dn = (((z + nz - 1) % nz) * 8 + q, ch)
    y_far = (base + plane(1 - y_lo, x), (1 - y_hi) * 2 + core)

    def half_rows(half):
        return pl.ds(pl.multiple_of(half * HALF, HALF), HALF)

    pairs = (
        (w_hbm, w_ref),
        (tok_hbm.at[half_rows(core), :], tok_ref.at[half_rows(core), :]),
        (gain_hbm, gain_ref),
        (tok_hbm.at[half_rows(1 - core), :], tok_ref.at[half_rows(1 - core), :]),
        (dec_hbm, dec_ref),
        (res_hbm, res_ref),
        (taps_hbm, taps_ref),
        (skip_hbm, skip_ref),
    )
    fetch = [pltpu.make_async_copy(a, b, in_sem.at[i]) for i, (a, b) in enumerate(pairs)]
    for copy in fetch:
        copy.start()

    totals[...] = jnp.zeros_like(totals)

    barrier = pltpu.get_barrier_semaphore()

    def greet(dev):
        pl.semaphore_signal(barrier, inc=1, device_id=dev, device_id_type=MESH)

    @pl.loop(1, GROUP)
    def _(d):
        greet((base + (q + d) % 8, ch))
        greet((base + (q + d) % 8, y_hi * 2 + (1 - core)))

    greet(z_up)
    greet(z_dn)
    greet(y_far)
    greet(sib)

    lane = lax.broadcasted_iota(jnp.int32, (8, LANES), 1)
    left = lane < HALF
    sub = lax.broadcasted_iota(jnp.int32, (8, LANES), 0)

    def swap(v):
        return pltpu.roll(v, HALF, 1)

    def pick(v, lf):
        r = swap(v)
        even = jnp.where(lf, v, r)
        odd = jnp.where(lf, r, v)
        return jnp.where(par == 0, even, odd)

    j_own = plane(y_lo, x)
    j_up = plane(y_lo, (x + 1) % 4)
    j_dn = plane(y_lo, (x + 3) % 4)
    j_op = plane(y_lo, (x + 2) % 4)
    p_own = plane(1 - y_lo, x)
    p_up = plane(1 - y_lo, (x + 1) % 4)
    p_dn = plane(1 - y_lo, (x + 3) % 4)
    p_op = plane(1 - y_lo, (x + 2) % 4)

    def norm(half, piece):
        rows = pl.ds(pl.multiple_of(half * HALF + piece * PIECE, PIECE), PIECE)
        v = tok_ref[rows, :].astype(F32)
        ms = jnp.mean(v * v, axis=1, keepdims=True)
        X[j_own, rows, :] = (v * lax.rsqrt(ms + 1e-06) * gain_ref[...]).astype(BF16)

    fetch[0].wait()
    left32 = lax.broadcasted_iota(jnp.int32, (32, LANES), 1) < HALF
    left16 = lax.broadcasted_iota(jnp.int32, (16, LANES), 1) < HALF
    for t in range(GROUP // 2):
        f0, f1, f2 = [w_ref[i, :, t * LANES : (t + 1) * LANES].astype(F32) for i in range(3)]
        r0, r1, r2 = swap(f0), swap(f1), swap(f2)
        wpack[2 * t, 0:32, :] = jnp.where(left32, f0, r1).astype(BF16)
        wpack[2 * t, 32:48, :] = jnp.where(left16, f2[0:16], r2[16:32]).astype(BF16)
        wpack[2 * t + 1, 0:32, :] = jnp.where(left32, r0, f1).astype(BF16)
        wpack[2 * t + 1, 32:48, :] = jnp.where(left16, r2[0:16], f2[16:32]).astype(BF16)
    fetch[1].wait()
    fetch[2].wait()
    norm(core, 0)
    norm(core, 2)
    pl.semaphore_wait(barrier, 7 + 7 + 2 + 2)

    sent = []

    def w_rows(c, chip):
        return slabs.at[c, z, pl.ds(pl.multiple_of(chip * 48, 16), 48), :]

    def wa_copy(d):
        to = (q + d) % 8
        return pltpu.make_async_remote_copy(
            src_ref=wpack.at[to],
            dst_ref=w_rows(core, q),
            send_sem=wa_send.at[d],
            recv_sem=wa_recv.at[core * 8 + d],
            device_id=(base + to, y_hi * 2 + 1),
            device_id_type=MESH,
        )

    @pl.loop(1, GROUP)
    def _(d):
        wa_copy(d).start()

    @pl.when(core == 0)
    def _():
        wa_copy(0).start()

    count = [0]

    def piece_ref(j, half, piece):
        return X.at[j, pl.ds(pl.multiple_of(half * HALF + piece * PIECE, PIECE), PIECE), :]

    def send(j, piece, dev):
        ref = piece_ref(j, core, piece)
        recv = (sib_recv if dev is sib else tok_recv).at[j * 4 + piece]
        copy = pltpu.make_async_remote_copy(
            src_ref=ref,
            dst_ref=ref,
            send_sem=tok_send.at[count[0]],
            recv_sem=recv,
            device_id=dev,
            device_id_type=MESH,
        )
        count[0] += 1
        sent.append(copy)
        return copy

    def arrive(j, piece):
        ref = piece_ref(j, core, piece)
        pltpu.make_async_remote_copy(
            src_ref=ref,
            dst_ref=ref,
            send_sem=tok_send.at[0],
            recv_sem=tok_recv.at[j * 4 + piece],
            device_id=sib,
            device_id_type=MESH,
        ).wait_recv()

    def arrive_sib(j, piece):
        ref = piece_ref(j, 1 - core, piece)
        pltpu.make_async_remote_copy(
            src_ref=ref,
            dst_ref=ref,
            send_sem=tok_send.at[0],
            recv_sem=sib_recv.at[j * 4 + piece],
            device_id=sib,
            device_id_type=MESH,
        ).wait_recv()

    send(j_own, 0, x_up).start()
    send(j_own, 2, x_dn).start()
    send(j_own, 0, y_up).start()
    send(j_own, 2, y_dn).start()
    norm(core, 1)
    norm(core, 3)
    send(j_own, 1, x_up).start()
    send(j_own, 3, x_dn).start()
    send(j_own, 1, y_up).start()
    send(j_own, 3, y_dn).start()
    send(j_own, 2, x_up).start()
    send(j_own, 0, x_dn).start()
    send(j_own, 3, x_up).start()
    send(j_own, 1, x_dn).start()

    CHUNK = 128
    last = nz // 2 - 1
    ways = (True, False)
    turns = [(c, k, up) for c in (1, 0) for k in range(3) for up in ways]

    def goes(step, up, c):
        return step < last or (step == last and c == (0 if up else 1))

    def z_copy(s, step, up, c, k):
        sems, recvs = (zp_send, zp_recv) if up else (zm_send, zm_recv)
        ref = slabs.at[c, s, pl.ds(k * CHUNK, CHUNK), :]
        return pltpu.make_async_remote_copy(
            src_ref=ref,
            dst_ref=ref,
            send_sem=sems.at[step * 6 + c * 3 + k],
            recv_sem=recvs.at[step * 6 + c * 3 + k],
            device_id=z_up if up else z_dn,
            device_id_type=MESH,
        )

    def z_out(step, up, c, k):
        return z_copy((z + nz - step) % nz if up else (z + step) % nz, step, up, c, k)

    def z_in(step, up, c, k):
        return z_copy(z_slab(step, up), step, up, c, k)

    def z_slab(step, up):
        return (z + 2 * nz - step - 1) % nz if up else (z + step + 1) % nz

    def hand_over(s, n):
        ref = slabs.at[0, s]
        return pltpu.make_async_remote_copy(
            src_ref=ref,
            dst_ref=ref,
            send_sem=sl_send.at[n],
            recv_sem=sl_recv.at[n],
            device_id=sib,
            device_id_type=MESH,
        )

    def came(step):
        if step < 0:
            return [(z, 15)]
        if step == last:
            return [(z_slab(step, True), step * 2)]
        return [(z_slab(step, up), step * 2 + (0 if up else 1)) for up in ways]

    @pl.when(core == 1)
    def _():
        slabs[1, z, pl.ds(pl.multiple_of(q * 48, 16), 48), :] = wpack[q]
        for c in (1, 0):
            for d in range(c, GROUP):
                ref = w_rows(c, (q + 8 - d) % 8)
                pltpu.make_async_remote_copy(
                    src_ref=ref,
                    dst_ref=ref,
                    send_sem=wa_send.at[d],
                    recv_sem=wa_recv.at[c * 8 + d],
                    device_id=sib,
                    device_id_type=MESH,
                ).wait_recv()
            for k in range(3):
                z_out(0, True, c, k).start()
                z_out(0, False, c, k).start()
        hand_over(z, 15).start()

    def unpack(s, n):
        @pl.when(core == 0)
        def _():
            hand_over(s, n).wait_recv()

        at = pl.multiple_of(s * 256, 256)
        for g in range(GROUP):
            v = slabs[core, s, g * 48 + 32 : g * 48 + 48, :]
            wfull[pl.ds(at + g * 32, 32), 0:LANES] = slabs[core, s, g * 48 : g * 48 + 32, :]
            wfull[pl.ds(at + g * 32, 16), LANES:] = v
            wfull[pl.ds(at + g * 32 + 16, 16), LANES:] = swap(v.astype(F32)).astype(BF16)

    def unpacks(step):
        return [functools.partial(unpack, s, n) for s, n in came(step)]

    def z_round(step, tasks):
        @pl.when(core == 1)
        def _():
            todo = list(tasks)
            for c, k, up in turns:
                if goes(step, up, c):
                    z_in(step, up, c, k).wait_recv()
                if goes(step + 1, up, c):
                    z_out(step + 1, up, c, k).start()
                if (c, k, up) == turns[-1]:
                    for s, n in came(step):
                        hand_over(s, n).start()
                if todo:
                    todo.pop(0)()
            for task in todo:
                task()

        @pl.when(core == 0)
        def _():
            for task in tasks:
                task()

    for copy in fetch[3:]:
        copy.wait()
    lanes_q = pl.ds(pl.multiple_of(tile * LANES, LANES), LANES)
    ones8 = jnp.ones((8, LANES), F32)
    subf = sub.astype(F32)

    def constants(first):
        dec = pick(dec_ref[:, lanes_q], left16)
        amp = pick(res_ref[:, lanes_q], left16) * jnp.sqrt(2.0 * dec)
        for s in (first, first + 1):
            d8 = dec[s : s + 1, :] * ones8
            amp_s[s] = amp[s : s + 1, :] * ones8
            lam_s[s] = jnp.exp(-d8)
            l62_s[s] = jnp.exp(-d8 * 62.0)
            l64_s[s] = jnp.exp(-d8 * 64.0)
            for i, sh in enumerate((1, 2, 4)):
                step_s[i, s] = jnp.where(sub >= sh, jnp.exp(-d8 * (128.0 * sh)), 0.0)
            pow_s[s] = jnp.exp(-d8 * (128.0 * subf))

    def z_weights():
        dec = pick(dec_ref[:, lanes_q], left16)
        dec_p = jnp.where(left, dec[0:8, :], dec[8:16, :])
        for s in range(nz):
            gap = (z - 1 - s).astype(F32)
            zw_s[s] = jnp.where(s < z, jnp.exp(-dec_p * (1024.0 * jnp.maximum(gap, 0.0))), 0.0)

    left64 = lax.broadcasted_iota(jnp.int32, (HALF, LANES), 1) < HALF

    def products(j, steps):
        acc = None
        for d in steps:
            at = pl.multiple_of(((z + nz + d) % nz) * 256, 256)
            term = jnp.dot(X[j, :, pl.ds(at, 256)], wfull[pl.ds(at, 256), :], preferred_element_type=F32)
            acc = term if acc is None else acc + term
        return acc

    def here(j):
        for piece in range(4):
            arrive_sib(j, piece)

    def add_products(j, steps, first):
        if first and j is not j_own:
            here(j)
        acc = products(j, steps)
        part[j] = acc if first else part[j] + acc

    done = {}

    def product_tasks(j, reach, each=3):
        steps = sorted(range(-reach, reach + 1), key=abs)
        done[id(j)] = steps
        return [
            functools.partial(add_products, j, steps[i : i + each], i == 0) for i in range(0, len(steps), each)
        ]

    def finish(j, acc):
        t0a, t0b = acc[0:HALF, 0:LANES], acc[HALF:, 0:LANES]
        t1a, t1b = acc[0:HALF, LANES:], acc[HALF:, LANES:]
        rows = half_rows(j)
        for i, v in enumerate(
            (
                jnp.where(left64, t0a, swap(t0b)),
                jnp.where(left64, swap(t0a), t0b),
                jnp.where(left64, t1a, swap(t1b)),
            )
        ):
            proj[i, rows, :] = v.astype(BF16).astype(F32)

    units = [
        [(j_dn, 0, (x_up, y_up)), (j_up, 2, (x_dn, y_dn)), (p_own, 0, ()), (p_own, 2, ())],
        [(j_dn, 1, (x_up, y_up)), (j_up, 3, (x_dn, y_dn)), (p_own, 1, ()), (p_own, 3, ())],
        [(j_dn, 2, (y_dn,)), (j_up, 0, (y_up,)), (p_dn, 0, ()), (p_up, 2, ())],
        [(j_dn, 3, (y_dn,)), (j_up, 1, (y_up,)), (p_dn, 1, (x_up,)), (p_up, 3, (x_dn,))],
        [(j_op, 0, (y_up,)), (j_op, 2, (y_dn,)), (p_up, 0, ()), (p_dn, 2, ())],
        [(j_op, 1, ()), (j_op, 3, ()), (p_up, 1, ()), (p_dn, 3, ())],
        [(p_op, 0, ()), (p_op, 2, ()), (p_op, 1, ()), (p_op, 3, ())],
    ]
    waiting = []

    def unit(u):
        for j, piece, onward in units[u]:
            arrive(j, piece)
            for dev in onward:
                send(j, piece, dev).start()
            waiting.append((j, piece))

    def to_sibling():
        tasks = [send(j, piece, sib).start for j, piece in waiting]
        waiting.clear()
        return tasks

    def more(reach, *blocks):
        for j in blocks:
            done[id(j)] = done[id(j)] + [reach, -reach]
        return [functools.partial(add_products, j, [reach, -reach], False) for j in blocks]

    def consts(*firsts):
        return [functools.partial(constants, s) for s in firsts]

    for piece in range(4):
        norm(1 - core, piece)
    unit(0)
    z_round(0, to_sibling() + unpacks(-1) + consts(0, 2))
    unit(1)
    z_round(1, to_sibling() + unpacks(0) + consts(4, 6, 8))
    unit(2)
    z_round(2, to_sibling() + unpacks(1) + consts(10, 12, 14))
    z_round(3, unpacks(2) + [z_weights])
    unit(3)
    z_round(4, to_sibling() + unpacks(3) + product_tasks(j_own, 4))
    unit(4)
    z_round(5, to_sibling() + unpacks(4) + more(5, j_own) + product_tasks(p_own, 5))
    unit(5)
    z_round(6, to_sibling() + unpacks(5) + more(6, j_own, p_own) + product_tasks(j_dn, 6) + product_tasks(j_up, 6))
    unit(6)
    for task in to_sibling():
        task()
    z_round(
        7,
        unpacks(6)
        + more(7, j_own, p_own, j_dn, j_up)
        + product_tasks(j_op, 7)
        + product_tasks(p_up, 7)
        + product_tasks(p_dn, 7)
        + product_tasks(p_op, 7),
    )
    for task in unpacks(7):
        task()
    for j in (j_own, p_own, j_dn, j_up, j_op, p_up, p_dn, p_op):
        finish(j, part[j] + products(j, [d for d in range(-8, 8) if d not in done[id(j)]]))

    rim_copy = pltpu.make_async_remote_copy(
        src_ref=proj.at[:, 504:512, :],
        dst_ref=rim,
        send_sem=rim_sem.at[0],
        recv_sem=rim_sem.at[1],
        device_id=z_up,
        device_id_type=MESH,
    )
    rim_copy.start()

    def at_step(i, r):
        return proj[i, pl.ds(r, 8, stride=HALF), :]

    def before(i, back, edge):
        last = swap(at_step(i, HALF - back))
        shifted = jnp.where(sub == 0, edge, pltpu.roll(last, 1, 0))
        return jnp.where(left, shifted, last)

    taps = [[pick(taps_ref[k, i : i + 1, lanes_q] * ones8, left) for i in range(3)] for k in range(3)]
    skp = pick(skip_ref[:, lanes_q] * ones8, left)

    def featurize(now, one, two):
        return [taps[0][i] * now[i] + taps[1][i] * one[i] + taps[2][i] * two[i] for i in range(3)]

    def scan_one(r, carry):
        one, two, states = carry
        now = [at_step(i, r) for i in range(3)]
        feats = featurize(now, one, two)
        drive = feats[1] * feats[2]
        drive_s[r] = drive
        gate_s[r] = feats[0]
        states = [lam_s[s] * states[s] + drive for s in range(MODES)]
        return now, one, states

    start = (
        [before(i, 1, 0.0) for i in range(3)],
        [before(i, 2, 0.0) for i in range(3)],
        [jnp.zeros((8, LANES), F32)] * MODES,
    )
    ends = lax.fori_loop(0, HALF, scan_one, start, unroll=2)[2]

    rim_copy.wait_recv()

    def edge(i, back):
        return jnp.where(z == 0, 0.0, swap(rim[i, 8 - back : 9 - back, :] * ones8))

    one = [before(i, 1, edge(i, 1)) for i in range(3)]
    two = [before(i, 2, edge(i, 2)) for i in range(3)]
    now = [at_step(i, 0) for i in range(3)]
    changes = []
    for r in range(2):
        feats = featurize(now, one, two)
        drive = feats[1] * feats[2]
        changes.append(drive - drive_s[r])
        drive_s[r] = drive
        gate_s[r] = feats[0]
        two, one, now = one, now, [at_step(i, 1) for i in range(3)]

    for s in range(MODES):
        e = ends[s] + l62_s[s] * (lam_s[s] * changes[0] + changes[1])
        sw = swap(e)
        el = jnp.where(left, e, sw)
        er = jnp.where(left, sw, e)
        g = l64_s[s] * el + er
        for i, sh in enumerate((1, 2, 4)):
            g = g + step_s[i, s] * pltpu.roll(g, sh, 0)
        end_s[0, s] = jnp.where(sub >= 1, pltpu.roll(g, 1, 0), 0.0)
        end_s[1, s] = el
        end_s[2, s] = g
    low = jnp.concatenate([end_s[2, s, 7:8, :] for s in range(8)], axis=0)
    high = jnp.concatenate([end_s[2, s, 7:8, :] for s in range(8, 16)], axis=0)
    totals[z] = jnp.where(left, low, high)

    def st_copy(d):
        return pltpu.make_async_remote_copy(
            src_ref=totals.at[z],
            dst_ref=totals.at[z],
            send_sem=st_send.at[d],
            recv_sem=st_recv.at[d],
            device_id=(((z + d) % nz) * 8 + q, ch),
            device_id_type=MESH,
        )

    far_first = sorted(range(1, nz), key=lambda d: -min(d, nz - d))
    for d in far_first:

        @pl.when(z + d < nz)
        def _(d=d):
            st_copy(d).start()

    for copy in sent:
        copy.wait_send()
    rim_copy.wait_send()

    @pl.loop(1, GROUP)
    def _(d):
        wa_copy(d).wait_send()

    @pl.when(core == 0)
    def _():
        wa_copy(0).wait_send()

    @pl.when(core == 1)
    def _():
        for step in range(last + 1):
            for c, k, up in turns:
                if goes(step, up, c):
                    z_out(step, up, c, k).wait_send()
        for step in range(-1, last + 1):
            for s, n in came(step):
                hand_over(s, n).wait_send()

    for d in range(1, nz):

        @pl.when(z >= d)
        def _(d=d):
            s = (z + nz - d) % nz
            pltpu.make_async_remote_copy(
                src_ref=totals.at[s],
                dst_ref=totals.at[s],
                send_sem=st_send.at[d],
                recv_sem=st_recv.at[d],
                device_id=sib,
                device_id_type=MESH,
            ).wait_recv()

    into = jnp.zeros((8, LANES), F32)
    for s in range(nz):
        into = into + zw_s[s] * totals[s]
    into_r = swap(into)
    into_lo = jnp.where(left, into, into_r)
    into_hi = jnp.where(left, into_r, into)

    states = []
    for s in range(MODES):
        zc = (into_lo if s < 8 else into_hi)[s % 8 : s % 8 + 1, :]
        c = end_s[0, s] + pow_s[s] * zc
        states.append(jnp.where(left, c, l64_s[s] * c + end_s[1, s]))

    def scan_two(r, states):
        drive = drive_s[r]
        states = [lam_s[s] * states[s] + drive for s in range(MODES)]
        terms = [amp_s[s] * states[s] for s in range(MODES)]
        while len(terms) > 1:
            terms = [a + b for a, b in zip(terms[::2], terms[1::2])]
        obuf[pl.ds(pl.multiple_of(r * 8, 8), 8), :] = gate_s[r] * (terms[0] + skp * drive)
        return states

    lax.fori_loop(0, HALF, scan_two, states, unroll=2)

    for j in range(GROUP):
        outbuf[j] = obuf[pl.ds(j, HALF, stride=8), :].astype(BF16)

    def out_copy(d):
        to = (q + d) % 8
        return pltpu.make_async_remote_copy(
            src_ref=outbuf.at[to],
            dst_ref=inbox.at[q],
            send_sem=out_send.at[d],
            recv_sem=out_recv.at[d],
            device_id=(base + to, ch),
            device_id_type=MESH,
        )

    for d in (6, 2, 7, 5, 3, 1, 4):
        out_copy(d).start()

    inbox[q] = outbuf[q]

    for d in range(1, nz):

        @pl.when(z + d < nz)
        def _(d=d):
            st_copy(d).wait_send()

    @pl.loop(1, GROUP)
    def _(d):
        ref = inbox.at[(q + 8 - d) % 8]
        pltpu.make_async_remote_copy(
            src_ref=ref,
            dst_ref=ref,
            send_sem=out_send.at[d],
            recv_sem=out_recv.at[d],
            device_id=sib,
            device_id_type=MESH,
        ).wait_recv()
        out_copy(d).wait_send()

    for g in range(GROUP // 2):
        a = inbox[2 * g].astype(F32)
        b = inbox[2 * g + 1].astype(F32)
        cols = slice(g * LANES, (g + 1) * LANES)
        o_ref[0:HALF, cols] = jnp.where(left64, a, swap(b)).astype(BF16)
        o_ref[HALF:, cols] = jnp.where(left64, swap(a), b).astype(BF16)


def local(tokens, norm_gain, in_proj, short_taps, decay, residue, skip):
    rows, width = tokens.shape
    channels = in_proj.shape[2]
    nz = lax.axis_size("ctx") // GROUP
    weights = jnp.transpose(in_proj, (1, 0, 2))
    vmem = pl.BlockSpec(memory_space=pltpu.VMEM)
    dma = pltpu.SemaphoreType.DMA
    const = pltpu.VMEM((MODES, 8, LANES), F32)
    return pl.pallas_call(
        functools.partial(kernel, nz),
        out_shape=jax.ShapeDtypeStruct((rows, channels), BF16),
        in_specs=[pl.BlockSpec(memory_space=pl.ANY)] * 7,
        out_specs=vmem,
        scratch_shapes=[
            pltpu.VMEM((rows, width), BF16),
            pltpu.VMEM((1, width), F32),
            pltpu.VMEM((3, 32, channels), BF16),
            pltpu.VMEM((3, 3, channels), F32),
            pltpu.VMEM((MODES, channels), F32),
            pltpu.VMEM((MODES, channels), F32),
            pltpu.VMEM((1, channels), F32),
            pltpu.VMEM((GROUP, ROWS, width), BF16),
            pltpu.VMEM((GROUP, 48, LANES), BF16),
            pltpu.VMEM((2, nz, 384, LANES), BF16),
            pltpu.VMEM((width, 2 * LANES), BF16),
            pltpu.VMEM((GROUP, ROWS, 2 * LANES), F32),
            pltpu.VMEM((3, GROUP * HALF, LANES), F32),
            pltpu.VMEM((3, 8, LANES), F32),
            pltpu.VMEM((HALF, 8, LANES), F32),
            pltpu.VMEM((HALF, 8, LANES), F32),
            const,
            const,
            const,
            const,
            pltpu.VMEM((3, MODES, 8, LANES), F32),
            const,
            pltpu.VMEM((nz, 8, LANES), F32),
            pltpu.VMEM((3, MODES, 8, LANES), F32),
            pltpu.VMEM((nz, 8, LANES), F32),
            pltpu.VMEM((GROUP * HALF, LANES), F32),
            pltpu.VMEM((GROUP, HALF, LANES), BF16),
            pltpu.VMEM((GROUP, HALF, LANES), BF16),
            dma((8,)),
            dma((8,)),
            dma((16,)),
            dma((64,)),
            dma((32,)),
            dma((32,)),
            dma((48,)),
            dma((48,)),
            dma((48,)),
            dma((48,)),
            dma((16,)),
            dma((16,)),
            dma((2,)),
            dma((16,)),
            dma((16,)),
            dma((8,)),
            dma((8,)),
        ],
        compiler_params=pltpu.CompilerParams(
            collective_id=0, has_side_effects=True, vmem_limit_bytes=56 * 1024 * 1024
        ),
        name="hyena",
    )(
        tokens,
        norm_gain.reshape(1, width),
        weights,
        short_taps,
        decay,
        residue,
        skip.reshape(1, channels),
    )


def solution(mesh):
    placed = (
        P("ctx", None),
        P(),
        P("ctx", None, "ch"),
        P(None, None, "ch"),
        P(None, "ch"),
        P(None, "ch"),
        P("ch"),
    )
    return jax.shard_map(
        local, mesh=mesh, in_specs=placed, out_specs=P("ctx", "ch"), check_vma=False
    )
```

```python
import functools

import jax
import jax.numpy as jnp
from jax import lax
from jax.experimental import pallas as pl
from jax.experimental.pallas import tpu as pltpu
from jax.sharding import PartitionSpec as P

MESH = pl.DeviceIdType.MESH
F32 = jnp.float32
BF16 = jnp.bfloat16

ROWS = 128
GROUP = 8
PIECE = 16
LANES = 128
HALF = 64
MODES = 16


def kernel(
    nz,
    tok_hbm,
    gain_hbm,
    w_hbm,
    taps_hbm,
    dec_hbm,
    res_hbm,
    skip_hbm,
    o_ref,
    tok_ref,
    gain_ref,
    w_ref,
    taps_ref,
    dec_ref,
    res_ref,
    skip_ref,
    X,
    wpack,
    slabs,
    wfull,
    part,
    proj,
    rim,
    drive_s,
    gate_s,
    lam_s,
    amp_s,
    l62_s,
    l64_s,
    step_s,
    pow_s,
    zw_s,
    end_s,
    totals,
    obuf,
    outbuf,
    inbox,
    in_sem,
    wa_send,
    wa_recv,
    tok_send,
    tok_recv,
    sib_recv,
    zp_send,
    zp_recv,
    zm_send,
    zm_recv,
    sl_send,
    sl_recv,
    rim_sem,
    st_send,
    st_recv,
    out_send,
    out_recv,
):
    ctx = lax.axis_index("ctx")
    ch = lax.axis_index("ch")
    z = ctx // 8
    q = ctx % 8
    y_lo = q // 4
    x = q % 4
    y_hi = ch // 2
    core = ch % 2
    par = q % 2
    tile = q // 2
    base = z * 8

    def plane(yl, xx):
        return yl * 4 + xx

    x_up = (base + plane(y_lo, (x + 1) % 4), ch)
    x_dn = (base + plane(y_lo, (x + 3) % 4), ch)
    y = y_hi * 2 + y_lo
    y_a = (y + 1) % 4
    y_b = (y + 3) % 4
    y_up = (base + plane(y_a % 2, x), (y_a // 2) * 2 + core)
    y_dn = (base + plane(y_b % 2, x), (y_b // 2) * 2 + core)
    sib = (ctx, y_hi * 2 + (1 - core))
    z_up = (((z + 1) % nz) * 8 + q, ch)
    z_dn = (((z + nz - 1) % nz) * 8 + q, ch)
    y_far = (base + plane(1 - y_lo, x), (1 - y_hi) * 2 + core)

    def half_rows(half):
        return pl.ds(pl.multiple_of(half * HALF, HALF), HALF)

    pairs = (
        (w_hbm, w_ref),
        (tok_hbm.at[half_rows(core), :], tok_ref.at[half_rows(core), :]),
        (gain_hbm, gain_ref),
        (tok_hbm.at[half_rows(1 - core), :], tok_ref.at[half_rows(1 - core), :]),
        (dec_hbm, dec_ref),
        (res_hbm, res_ref),
        (taps_hbm, taps_ref),
        (skip_hbm, skip_ref),
    )
    fetch = [pltpu.make_async_copy(a, b, in_sem.at[i]) for i, (a, b) in enumerate(pairs)]
    for copy in fetch:
        copy.start()

    totals[...] = jnp.zeros_like(totals)

    barrier = pltpu.get_barrier_semaphore()

    def greet(dev):
        pl.semaphore_signal(barrier, inc=1, device_id=dev, device_id_type=MESH)

    @pl.when(core == 1)
    def _():
        @pl.loop(1, GROUP)
        def _(d):
            greet((base + (q + d) % 8, ch))
            greet((base + (q + d) % 8, y_hi * 2))

        greet(z_up)
        greet(z_dn)
        greet(y_far)

    @pl.when(core == 0)
    def _():
        for dev in (x_up, x_dn, y_up, y_dn):
            greet(dev)

    greet(sib)

    lane = lax.broadcasted_iota(jnp.int32, (8, LANES), 1)
    left = lane < HALF
    sub = lax.broadcasted_iota(jnp.int32, (8, LANES), 0)

    def swap(v):
        return pltpu.roll(v, HALF, 1)

    def pick(v, lf):
        r = swap(v)
        even = jnp.where(lf, v, r)
        odd = jnp.where(lf, r, v)
        return jnp.where(par == 0, even, odd)

    j_own = plane(y_lo, x)
    j_up = plane(y_lo, (x + 1) % 4)
    j_dn = plane(y_lo, (x + 3) % 4)
    j_op = plane(y_lo, (x + 2) % 4)
    p_own = plane(1 - y_lo, x)
    p_up = plane(1 - y_lo, (x + 1) % 4)
    p_dn = plane(1 - y_lo, (x + 3) % 4)
    p_op = plane(1 - y_lo, (x + 2) % 4)

    def norm(half, piece):
        rows = pl.ds(pl.multiple_of(half * HALF + piece * PIECE, PIECE), PIECE)
        v = tok_ref[rows, :].astype(F32)
        ms = jnp.mean(v * v, axis=1, keepdims=True)
        X[j_own, rows, :] = (v * lax.rsqrt(ms + 1e-06) * gain_ref[...]).astype(BF16)

    fetch[0].wait()
    left32 = lax.broadcasted_iota(jnp.int32, (32, LANES), 1) < HALF
    left16 = lax.broadcasted_iota(jnp.int32, (16, LANES), 1) < HALF
    for t in range(GROUP // 2):
        f0, f1, f2 = [w_ref[i, :, t * LANES : (t + 1) * LANES].astype(F32) for i in range(3)]
        r0, r1, r2 = swap(f0), swap(f1), swap(f2)
        wpack[2 * t, 0:32, :] = jnp.where(left32, f0, r1).astype(BF16)
        wpack[2 * t, 32:48, :] = jnp.where(left16, f2[0:16], r2[16:32]).astype(BF16)
        wpack[2 * t + 1, 0:32, :] = jnp.where(left32, r0, f1).astype(BF16)
        wpack[2 * t + 1, 32:48, :] = jnp.where(left16, r2[0:16], f2[16:32]).astype(BF16)
    fetch[1].wait()
    fetch[2].wait()
    norm(core, 0)
    norm(core, 2)
    pl.semaphore_wait(barrier, 12 - core)

    sent = []

    def w_rows(c, chip):
        return slabs.at[c, z, pl.ds(pl.multiple_of(chip * 48, 16), 48), :]

    def wa_copy(d):
        to = (q + d) % 8
        return pltpu.make_async_remote_copy(
            src_ref=wpack.at[to],
            dst_ref=w_rows(core, q),
            send_sem=wa_send.at[d],
            recv_sem=wa_recv.at[core * 8 + d],
            device_id=(base + to, y_hi * 2 + 1),
            device_id_type=MESH,
        )

    @pl.loop(1, GROUP)
    def _(d):
        wa_copy(d).start()

    @pl.when(core == 0)
    def _():
        wa_copy(0).start()

    count = [0]

    def piece_ref(j, half, piece):
        return X.at[j, pl.ds(pl.multiple_of(half * HALF + piece * PIECE, PIECE), PIECE), :]

    def send(j, piece, dev):
        ref = piece_ref(j, core, piece)
        recv = (sib_recv if dev is sib else tok_recv).at[j * 4 + piece]
        copy = pltpu.make_async_remote_copy(
            src_ref=ref,
            dst_ref=ref,
            send_sem=tok_send.at[count[0]],
            recv_sem=recv,
            device_id=dev,
            device_id_type=MESH,
        )
        count[0] += 1
        sent.append(copy)
        return copy

    def arrive(j, piece):
        ref = piece_ref(j, core, piece)
        pltpu.make_async_remote_copy(
            src_ref=ref,
            dst_ref=ref,
            send_sem=tok_send.at[0],
            recv_sem=tok_recv.at[j * 4 + piece],
            device_id=sib,
            device_id_type=MESH,
        ).wait_recv()

    def arrive_sib(j, piece):
        ref = piece_ref(j, 1 - core, piece)
        pltpu.make_async_remote_copy(
            src_ref=ref,
            dst_ref=ref,
            send_sem=tok_send.at[0],
            recv_sem=sib_recv.at[j * 4 + piece],
            device_id=sib,
            device_id_type=MESH,
        ).wait_recv()

    send(j_own, 0, x_up).start()
    send(j_own, 2, x_dn).start()
    send(j_own, 0, y_up).start()
    send(j_own, 2, y_dn).start()
    norm(core, 1)
    norm(core, 3)
    send(j_own, 1, x_up).start()
    send(j_own, 3, x_dn).start()
    send(j_own, 1, y_up).start()
    send(j_own, 3, y_dn).start()
    send(j_own, 2, x_up).start()
    send(j_own, 0, x_dn).start()
    send(j_own, 3, x_up).start()
    send(j_own, 1, x_dn).start()

    CHUNK = 128
    last = nz // 2 - 1
    ways = (True, False)
    turns = [(c, k, up) for c in (1, 0) for k in range(3) for up in ways]

    def goes(step, up, c):
        return step < last or (step == last and c == (0 if up else 1))

    def z_copy(s, step, up, c, k):
        sems, recvs = (zp_send, zp_recv) if up else (zm_send, zm_recv)
        ref = slabs.at[c, s, pl.ds(k * CHUNK, CHUNK), :]
        return pltpu.make_async_remote_copy(
            src_ref=ref,
            dst_ref=ref,
            send_sem=sems.at[step * 6 + c * 3 + k],
            recv_sem=recvs.at[step * 6 + c * 3 + k],
            device_id=(z_up[0], y_hi * 2) if straight(step, up, c) else z_up if up else z_dn,
            device_id_type=MESH,
        )

    def straight(step, up, c):
        return step == last and up and c == 0

    def z_out(step, up, c, k):
        return z_copy((z + nz - step) % nz if up else (z + step) % nz, step, up, c, k)

    def z_in(step, up, c, k):
        return z_copy(z_slab(step, up), step, up, c, k)

    def z_slab(step, up):
        return (z + 2 * nz - step - 1) % nz if up else (z + step + 1) % nz

    def hand_over(s, n):
        ref = slabs.at[0, s]
        return pltpu.make_async_remote_copy(
            src_ref=ref,
            dst_ref=ref,
            send_sem=sl_send.at[n],
            recv_sem=sl_recv.at[n],
            device_id=sib,
            device_id_type=MESH,
        )

    def came(step):
        if step < 0:
            return [(z, 15)]
        if step == last:
            return [(z_slab(step, True), step * 2)]
        return [(z_slab(step, up), step * 2 + (0 if up else 1)) for up in ways]

    @pl.when(core == 1)
    def _():
        slabs[1, z, pl.ds(pl.multiple_of(q * 48, 16), 48), :] = wpack[q]
        for c in (1, 0):
            for d in range(c, GROUP):
                ref = w_rows(c, (q + 8 - d) % 8)
                pltpu.make_async_remote_copy(
                    src_ref=ref,
                    dst_ref=ref,
                    send_sem=wa_send.at[d],
                    recv_sem=wa_recv.at[c * 8 + d],
                    device_id=sib,
                    device_id_type=MESH,
                ).wait_recv()
            for k in range(3):
                z_out(0, True, c, k).start()
                z_out(0, False, c, k).start()
        hand_over(z, 15).start()

    def unpack(s, n):
        @pl.when(core == 0)
        def _():
            if n == 2 * last:
                for k in range(3):
                    z_in(last, True, 0, k).wait_recv()
            else:
                hand_over(s, n).wait_recv()

        at = pl.multiple_of(s * 256, 256)
        for g in range(GROUP):
            v = slabs[core, s, g * 48 + 32 : g * 48 + 48, :]
            wfull[pl.ds(at + g * 32, 32), 0:LANES] = slabs[core, s, g * 48 : g * 48 + 32, :]
            wfull[pl.ds(at + g * 32, 16), LANES:] = v
            wfull[pl.ds(at + g * 32 + 16, 16), LANES:] = swap(v.astype(F32)).astype(BF16)

    def unpacks(step):
        return [functools.partial(unpack, s, n) for s, n in came(step)]

    def z_round(step, tasks):
        @pl.when(core == 1)
        def _():
            todo = list(tasks)
            for c, k, up in turns:
                if goes(step, up, c) and not straight(step, up, c):
                    z_in(step, up, c, k).wait_recv()
                if goes(step + 1, up, c):
                    z_out(step + 1, up, c, k).start()
                if (c, k, up) == turns[-1] and step < last:
                    for s, n in came(step):
                        hand_over(s, n).start()
                if todo:
                    todo.pop(0)()
            for task in todo:
                task()

        @pl.when(core == 0)
        def _():
            for task in tasks:
                task()

    for copy in fetch[3:]:
        copy.wait()
    lanes_q = pl.ds(pl.multiple_of(tile * LANES, LANES), LANES)
    ones8 = jnp.ones((8, LANES), F32)
    subf = sub.astype(F32)

    def constants(first):
        dec = pick(dec_ref[:, lanes_q], left16)
        amp = pick(res_ref[:, lanes_q], left16) * jnp.sqrt(2.0 * dec)
        for s in (first, first + 1):
            d8 = dec[s : s + 1, :] * ones8
            amp_s[s] = amp[s : s + 1, :] * ones8
            lam_s[s] = jnp.exp(-d8)
            l62_s[s] = jnp.exp(-d8 * 62.0)
            l64_s[s] = jnp.exp(-d8 * 64.0)
            for i, sh in enumerate((1, 2, 4)):
                step_s[i, s] = jnp.where(sub >= sh, jnp.exp(-d8 * (128.0 * sh)), 0.0)
            pow_s[s] = jnp.exp(-d8 * (128.0 * subf))

    def z_weights():
        dec = pick(dec_ref[:, lanes_q], left16)
        dec_p = jnp.where(left, dec[0:8, :], dec[8:16, :])
        for s in range(nz):
            gap = (z - 1 - s).astype(F32)
            zw_s[s] = jnp.where(s < z, jnp.exp(-dec_p * (1024.0 * jnp.maximum(gap, 0.0))), 0.0)

    left64 = lax.broadcasted_iota(jnp.int32, (HALF, LANES), 1) < HALF

    def products(j, steps):
        acc = None
        for d in steps:
            at = pl.multiple_of(((z + nz + d) % nz) * 256, 256)
            term = jnp.dot(X[j, :, pl.ds(at, 256)], wfull[pl.ds(at, 256), :], preferred_element_type=F32)
            acc = term if acc is None else acc + term
        return acc

    def here(j):
        for piece in range(4):
            arrive_sib(j, piece)

    def add_products(j, steps, first):
        if first and j is not j_own:
            here(j)
        acc = products(j, steps)
        part[j] = acc if first else part[j] + acc

    def product_tasks(j, reach, each=3):
        steps = sorted(range(-reach, reach + 1), key=abs)
        return [
            functools.partial(add_products, j, steps[i : i + each], i == 0) for i in range(0, len(steps), each)
        ]

    def finish(j, acc):
        t0a, t0b = acc[0:HALF, 0:LANES], acc[HALF:, 0:LANES]
        t1a, t1b = acc[0:HALF, LANES:], acc[HALF:, LANES:]
        rows = half_rows(j)
        for i, v in enumerate(
            (
                jnp.where(left64, t0a, swap(t0b)),
                jnp.where(left64, swap(t0a), t0b),
                jnp.where(left64, t1a, swap(t1b)),
            )
        ):
            proj[i, rows, :] = v.astype(BF16).astype(F32)

    units = [
        [(j_dn, 0, (x_up, y_up)), (j_up, 2, (x_dn, y_dn)), (p_own, 0, ()), (p_own, 2, ())],
        [(j_dn, 1, (x_up, y_up)), (j_up, 3, (x_dn, y_dn)), (p_own, 1, ()), (p_own, 3, ())],
        [(j_dn, 2, (y_dn,)), (j_up, 0, (y_up,)), (p_dn, 0, ()), (p_up, 2, ())],
        [(j_dn, 3, (y_dn,)), (j_up, 1, (y_up,)), (p_dn, 1, (x_up,)), (p_up, 3, (x_dn,))],
        [(j_op, 0, (y_up,)), (j_op, 2, (y_dn,)), (p_up, 0, ()), (p_dn, 2, ())],
        [(j_op, 1, ()), (j_op, 3, ()), (p_up, 1, ()), (p_dn, 3, ())],
        [(p_op, 0, ()), (p_op, 2, ()), (p_op, 1, ()), (p_op, 3, ())],
    ]
    waiting = []

    def unit(u):
        for j, piece, onward in units[u]:
            arrive(j, piece)
            for dev in onward:
                send(j, piece, dev).start()
            waiting.append((j, piece))

    def to_sibling():
        tasks = [send(j, piece, sib).start for j, piece in waiting]
        waiting.clear()
        return tasks

    def more(reach, *blocks):
        return [functools.partial(add_products, j, [reach, -reach], False) for j in blocks]

    def consts(*firsts):
        return [functools.partial(constants, s) for s in firsts]

    for piece in range(4):
        norm(1 - core, piece)
    unit(0)
    z_round(0, to_sibling() + unpacks(-1) + consts(0, 2))
    unit(1)
    z_round(1, to_sibling() + unpacks(0) + consts(4, 6, 8))
    unit(2)
    z_round(2, to_sibling() + unpacks(1) + consts(10, 12, 14))
    z_round(3, unpacks(2) + [z_weights])
    unit(3)
    z_round(4, to_sibling() + unpacks(3) + product_tasks(j_own, 4))
    unit(4)
    z_round(5, to_sibling() + unpacks(4) + more(5, j_own) + product_tasks(p_own, 5))
    unit(5)
    z_round(6, to_sibling() + unpacks(5) + more(6, j_own, p_own) + product_tasks(j_dn, 6) + product_tasks(j_up, 6))
    unit(6)
    for task in to_sibling():
        task()
    z_round(
        7,
        unpacks(6)
        + more(7, j_own, p_own, j_dn, j_up)
        + product_tasks(j_op, 7)
        + product_tasks(p_up, 7)
        + product_tasks(p_dn, 7)
        + product_tasks(p_op, 7),
    )
    for task in unpacks(7):
        task()
    finish(7, part[7] + products(7, (-8,)))

    rim_copy = pltpu.make_async_remote_copy(
        src_ref=proj.at[:, 504:512, :],
        dst_ref=rim,
        send_sem=rim_sem.at[0],
        recv_sem=rim_sem.at[1],
        device_id=z_up,
        device_id_type=MESH,
    )
    rim_copy.start()
    for j in range(7):
        finish(j, part[j] + products(j, (-8,)))

    def at_step(i, r):
        return proj[i, pl.ds(r, 8, stride=HALF), :]

    def before(i, back, edge):
        last = swap(at_step(i, HALF - back))
        shifted = jnp.where(sub == 0, edge, pltpu.roll(last, 1, 0))
        return jnp.where(left, shifted, last)

    taps = [[pick(taps_ref[k, i : i + 1, lanes_q] * ones8, left) for i in range(3)] for k in range(3)]
    skp = pick(skip_ref[:, lanes_q] * ones8, left)

    def featurize(now, one, two):
        return [taps[0][i] * now[i] + taps[1][i] * one[i] + taps[2][i] * two[i] for i in range(3)]

    def scan_one(r, carry):
        one, two, states = carry
        now = [at_step(i, r) for i in range(3)]
        feats = featurize(now, one, two)
        drive = feats[1] * feats[2]
        drive_s[r] = drive
        gate_s[r] = feats[0]
        states = [lam_s[s] * states[s] + drive for s in range(MODES)]
        return now, one, states

    start = (
        [before(i, 1, 0.0) for i in range(3)],
        [before(i, 2, 0.0) for i in range(3)],
        [jnp.zeros((8, LANES), F32)] * MODES,
    )
    ends = lax.fori_loop(0, HALF, scan_one, start, unroll=4)[2]

    rim_copy.wait_recv()

    def edge(i, back):
        return jnp.where(z == 0, 0.0, swap(rim[i, 8 - back : 9 - back, :] * ones8))

    one = [before(i, 1, edge(i, 1)) for i in range(3)]
    two = [before(i, 2, edge(i, 2)) for i in range(3)]
    now = [at_step(i, 0) for i in range(3)]
    changes = []
    for r in range(2):
        feats = featurize(now, one, two)
        drive = feats[1] * feats[2]
        changes.append(drive - drive_s[r])
        drive_s[r] = drive
        gate_s[r] = feats[0]
        two, one, now = one, now, [at_step(i, 1) for i in range(3)]

    for s in range(MODES):
        e = ends[s] + l62_s[s] * (lam_s[s] * changes[0] + changes[1])
        sw = swap(e)
        el = jnp.where(left, e, sw)
        er = jnp.where(left, sw, e)
        g = l64_s[s] * el + er
        for i, sh in enumerate((1, 2, 4)):
            g = g + step_s[i, s] * pltpu.roll(g, sh, 0)
        end_s[0, s] = jnp.where(sub >= 1, pltpu.roll(g, 1, 0), 0.0)
        end_s[1, s] = el
        end_s[2, s] = g
    low = jnp.concatenate([end_s[2, s, 7:8, :] for s in range(8)], axis=0)
    high = jnp.concatenate([end_s[2, s, 7:8, :] for s in range(8, 16)], axis=0)
    totals[z] = jnp.where(left, low, high)

    def st_copy(d):
        return pltpu.make_async_remote_copy(
            src_ref=totals.at[z],
            dst_ref=totals.at[z],
            send_sem=st_send.at[d],
            recv_sem=st_recv.at[d],
            device_id=(((z + d) % nz) * 8 + q, ch),
            device_id_type=MESH,
        )

    far_first = sorted(range(1, nz), key=lambda d: -min(d, nz - d))
    for d in far_first:

        @pl.when(z + d < nz)
        def _(d=d):
            st_copy(d).start()

    for copy in sent:
        copy.wait_send()
    rim_copy.wait_send()

    @pl.loop(1, GROUP)
    def _(d):
        wa_copy(d).wait_send()

    @pl.when(core == 0)
    def _():
        wa_copy(0).wait_send()

    @pl.when(core == 1)
    def _():
        for step in range(last + 1):
            for c, k, up in turns:
                if goes(step, up, c):
                    z_out(step, up, c, k).wait_send()
        for step in range(-1, last):
            for s, n in came(step):
                hand_over(s, n).wait_send()

    for d in range(1, nz):

        @pl.when(z >= d)
        def _(d=d):
            s = (z + nz - d) % nz
            pltpu.make_async_remote_copy(
                src_ref=totals.at[s],
                dst_ref=totals.at[s],
                send_sem=st_send.at[d],
                recv_sem=st_recv.at[d],
                device_id=sib,
                device_id_type=MESH,
            ).wait_recv()

    into = jnp.zeros((8, LANES), F32)
    for s in range(nz):
        into = into + zw_s[s] * totals[s]
    into_r = swap(into)
    into_lo = jnp.where(left, into, into_r)
    into_hi = jnp.where(left, into_r, into)

    states = []
    for s in range(MODES):
        zc = (into_lo if s < 8 else into_hi)[s % 8 : s % 8 + 1, :]
        c = end_s[0, s] + pow_s[s] * zc
        states.append(jnp.where(left, c, l64_s[s] * c + end_s[1, s]))

    def scan_two(r, states):
        drive = drive_s[r]
        states = [lam_s[s] * states[s] + drive for s in range(MODES)]
        terms = [amp_s[s] * states[s] for s in range(MODES)]
        while len(terms) > 1:
            terms = [a + b for a, b in zip(terms[::2], terms[1::2])]
        obuf[pl.ds(pl.multiple_of(r * 8, 8), 8), :] = gate_s[r] * (terms[0] + skp * drive)
        return states

    lax.fori_loop(0, HALF, scan_two, states, unroll=4)

    for j in range(GROUP):
        outbuf[j] = obuf[pl.ds(j, HALF, stride=8), :].astype(BF16)

    def out_copy(d):
        to = (q + d) % 8
        return pltpu.make_async_remote_copy(
            src_ref=outbuf.at[to],
            dst_ref=inbox.at[q],
            send_sem=out_send.at[d],
            recv_sem=out_recv.at[d],
            device_id=(base + to, ch),
            device_id_type=MESH,
        )

    for d in (6, 2, 7, 5, 3, 1, 4):
        out_copy(d).start()

    inbox[q] = outbuf[q]

    for d in range(1, nz):

        @pl.when(z + d < nz)
        def _(d=d):
            st_copy(d).wait_send()

    @pl.loop(1, GROUP)
    def _(d):
        ref = inbox.at[(q + 8 - d) % 8]
        pltpu.make_async_remote_copy(
            src_ref=ref,
            dst_ref=ref,
            send_sem=out_send.at[d],
            recv_sem=out_recv.at[d],
            device_id=sib,
            device_id_type=MESH,
        ).wait_recv()
        out_copy(d).wait_send()

    for g in range(GROUP // 2):
        a = inbox[2 * g].astype(F32)
        b = inbox[2 * g + 1].astype(F32)
        cols = slice(g * LANES, (g + 1) * LANES)
        o_ref[0:HALF, cols] = jnp.where(left64, a, swap(b)).astype(BF16)
        o_ref[HALF:, cols] = jnp.where(left64, swap(a), b).astype(BF16)


def local(tokens, norm_gain, in_proj, short_taps, decay, residue, skip):
    rows, width = tokens.shape
    channels = in_proj.shape[2]
    nz = lax.axis_size("ctx") // GROUP
    weights = jnp.transpose(in_proj, (1, 0, 2))
    vmem = pl.BlockSpec(memory_space=pltpu.VMEM)
    dma = pltpu.SemaphoreType.DMA
    const = pltpu.VMEM((MODES, 8, LANES), F32)
    return pl.pallas_call(
        functools.partial(kernel, nz),
        out_shape=jax.ShapeDtypeStruct((rows, channels), BF16),
        in_specs=[pl.BlockSpec(memory_space=pl.ANY)] * 7,
        out_specs=vmem,
        scratch_shapes=[
            pltpu.VMEM((rows, width), BF16),
            pltpu.VMEM((1, width), F32),
            pltpu.VMEM((3, 32, channels), BF16),
            pltpu.VMEM((3, 3, channels), F32),
            pltpu.VMEM((MODES, channels), F32),
            pltpu.VMEM((MODES, channels), F32),
            pltpu.VMEM((1, channels), F32),
            pltpu.VMEM((GROUP, ROWS, width), BF16),
            pltpu.VMEM((GROUP, 48, LANES), BF16),
            pltpu.VMEM((2, nz, 384, LANES), BF16),
            pltpu.VMEM((width, 2 * LANES), BF16),
            pltpu.VMEM((GROUP, ROWS, 2 * LANES), F32),
            pltpu.VMEM((3, GROUP * HALF, LANES), F32),
            pltpu.VMEM((3, 8, LANES), F32),
            pltpu.VMEM((HALF, 8, LANES), F32),
            pltpu.VMEM((HALF, 8, LANES), F32),
            const,
            const,
            const,
            const,
            pltpu.VMEM((3, MODES, 8, LANES), F32),
            const,
            pltpu.VMEM((nz, 8, LANES), F32),
            pltpu.VMEM((3, MODES, 8, LANES), F32),
            pltpu.VMEM((nz, 8, LANES), F32),
            pltpu.VMEM((GROUP * HALF, LANES), F32),
            pltpu.VMEM((GROUP, HALF, LANES), BF16),
            pltpu.VMEM((GROUP, HALF, LANES), BF16),
            dma((8,)),
            dma((8,)),
            dma((16,)),
            dma((64,)),
            dma((32,)),
            dma((32,)),
            dma((48,)),
            dma((48,)),
            dma((48,)),
            dma((48,)),
            dma((16,)),
            dma((16,)),
            dma((2,)),
            dma((16,)),
            dma((16,)),
            dma((8,)),
            dma((8,)),
        ],
        compiler_params=pltpu.CompilerParams(
            collective_id=0, has_side_effects=True, vmem_limit_bytes=56 * 1024 * 1024
        ),
        name="hyena",
    )(
        tokens,
        norm_gain.reshape(1, width),
        weights,
        short_taps,
        decay,
        residue,
        skip.reshape(1, channels),
    )


def solution(mesh):
    placed = (
        P("ctx", None),
        P(),
        P("ctx", None, "ch"),
        P(None, None, "ch"),
        P(None, "ch"),
        P(None, "ch"),
        P("ch"),
    )
    return jax.shard_map(
        local, mesh=mesh, in_specs=placed, out_specs=P("ctx", "ch"), check_vma=False
    )
```

```python
import functools

import jax
import jax.numpy as jnp
from jax import lax
from jax.experimental import pallas as pl
from jax.experimental.pallas import tpu as pltpu
from jax.sharding import PartitionSpec as P

MESH = pl.DeviceIdType.MESH
F32 = jnp.float32
BF16 = jnp.bfloat16

ROWS = 128
GROUP = 8
PIECE = 16
LANES = 128
HALF = 64
MODES = 16


def kernel(
    nz,
    tok_hbm,
    gain_hbm,
    w_hbm,
    taps_hbm,
    dec_hbm,
    res_hbm,
    skip_hbm,
    o_ref,
    tok_ref,
    gain_ref,
    w_ref,
    taps_ref,
    dec_ref,
    res_ref,
    skip_ref,
    X,
    wpack,
    slabs,
    wfull,
    part,
    proj,
    rim,
    drive_s,
    gate_s,
    lam_s,
    amp_s,
    l62_s,
    l64_s,
    step_s,
    pow_s,
    zw_s,
    end_s,
    totals,
    obuf,
    outbuf,
    inbox,
    in_sem,
    wa_send,
    wa_recv,
    tok_send,
    tok_recv,
    sib_recv,
    zp_send,
    zp_recv,
    zm_send,
    zm_recv,
    sl_send,
    sl_recv,
    rim_sem,
    st_send,
    st_recv,
    out_send,
    out_recv,
):
    ctx = lax.axis_index("ctx")
    ch = lax.axis_index("ch")
    z = ctx // 8
    q = ctx % 8
    y_lo = q // 4
    x = q % 4
    y_hi = ch // 2
    core = ch % 2
    par = q % 2
    tile = q // 2
    base = z * 8

    def plane(yl, xx):
        return yl * 4 + xx

    x_up = (base + plane(y_lo, (x + 1) % 4), ch)
    x_dn = (base + plane(y_lo, (x + 3) % 4), ch)
    y = y_hi * 2 + y_lo
    y_a = (y + 1) % 4
    y_b = (y + 3) % 4
    y_up = (base + plane(y_a % 2, x), (y_a // 2) * 2 + core)
    y_dn = (base + plane(y_b % 2, x), (y_b // 2) * 2 + core)
    sib = (ctx, y_hi * 2 + (1 - core))
    z_up = (((z + 1) % nz) * 8 + q, ch)
    z_dn = (((z + nz - 1) % nz) * 8 + q, ch)
    y_far = (base + plane(1 - y_lo, x), (1 - y_hi) * 2 + core)

    def half_rows(half):
        return pl.ds(pl.multiple_of(half * HALF, HALF), HALF)

    pairs = (
        (w_hbm, w_ref),
        (tok_hbm.at[half_rows(core), :], tok_ref.at[half_rows(core), :]),
        (gain_hbm, gain_ref),
        (tok_hbm.at[half_rows(1 - core), :], tok_ref.at[half_rows(1 - core), :]),
        (dec_hbm, dec_ref),
        (res_hbm, res_ref),
        (taps_hbm, taps_ref),
        (skip_hbm, skip_ref),
    )
    fetch = [pltpu.make_async_copy(a, b, in_sem.at[i]) for i, (a, b) in enumerate(pairs)]
    for copy in fetch:
        copy.start()

    totals[...] = jnp.zeros_like(totals)

    barrier = pltpu.get_barrier_semaphore()

    def greet(dev):
        pl.semaphore_signal(barrier, inc=1, device_id=dev, device_id_type=MESH)

    @pl.when(core == 1)
    def _():
        @pl.loop(1, GROUP)
        def _(d):
            greet((base + (q + d) % 8, ch))
            greet((base + (q + d) % 8, y_hi * 2))

        greet(z_up)
        greet(z_dn)
        greet(y_far)

    @pl.when(core == 0)
    def _():
        for dev in (x_up, x_dn, y_up, y_dn):
            greet(dev)

    greet(sib)

    lane = lax.broadcasted_iota(jnp.int32, (8, LANES), 1)
    left = lane < HALF
    sub = lax.broadcasted_iota(jnp.int32, (8, LANES), 0)

    def swap(v):
        return pltpu.roll(v, HALF, 1)

    def pick(v, lf):
        r = swap(v)
        even = jnp.where(lf, v, r)
        odd = jnp.where(lf, r, v)
        return jnp.where(par == 0, even, odd)

    j_own = plane(y_lo, x)
    j_up = plane(y_lo, (x + 1) % 4)
    j_dn = plane(y_lo, (x + 3) % 4)
    j_op = plane(y_lo, (x + 2) % 4)
    p_own = plane(1 - y_lo, x)
    p_up = plane(1 - y_lo, (x + 1) % 4)
    p_dn = plane(1 - y_lo, (x + 3) % 4)
    p_op = plane(1 - y_lo, (x + 2) % 4)

    def norm(half, piece):
        rows = pl.ds(pl.multiple_of(half * HALF + piece * PIECE, PIECE), PIECE)
        v = tok_ref[rows, :].astype(F32)
        ms = jnp.mean(v * v, axis=1, keepdims=True)
        X[j_own, rows, :] = (v * lax.rsqrt(ms + 1e-06) * gain_ref[...]).astype(BF16)

    fetch[0].wait()
    left32 = lax.broadcasted_iota(jnp.int32, (32, LANES), 1) < HALF
    left16 = lax.broadcasted_iota(jnp.int32, (16, LANES), 1) < HALF
    for t in range(GROUP // 2):
        f0, f1, f2 = [w_ref[i, :, t * LANES : (t + 1) * LANES].astype(F32) for i in range(3)]
        r0, r1, r2 = swap(f0), swap(f1), swap(f2)
        wpack[2 * t, 0:32, :] = jnp.where(left32, f0, r1).astype(BF16)
        wpack[2 * t, 32:48, :] = jnp.where(left16, f2[0:16], r2[16:32]).astype(BF16)
        wpack[2 * t + 1, 0:32, :] = jnp.where(left32, r0, f1).astype(BF16)
        wpack[2 * t + 1, 32:48, :] = jnp.where(left16, r2[0:16], f2[16:32]).astype(BF16)
    fetch[1].wait()
    fetch[2].wait()
    norm(core, 0)
    norm(core, 2)
    pl.semaphore_wait(barrier, 12 - core)

    sent = []

    def w_rows(c, chip):
        return slabs.at[c, z, pl.ds(pl.multiple_of(chip * 48, 16), 48), :]

    def wa_copy(d):
        to = (q + d) % 8
        return pltpu.make_async_remote_copy(
            src_ref=wpack.at[to],
            dst_ref=w_rows(core, q),
            send_sem=wa_send.at[d],
            recv_sem=wa_recv.at[core * 8 + d],
            device_id=(base + to, y_hi * 2 + 1),
            device_id_type=MESH,
        )

    @pl.loop(1, GROUP)
    def _(d):
        wa_copy(d).start()

    @pl.when(core == 0)
    def _():
        wa_copy(0).start()

    count = [0]

    def piece_ref(j, half, piece):
        return X.at[j, pl.ds(pl.multiple_of(half * HALF + piece * PIECE, PIECE), PIECE), :]

    def send(j, piece, dev):
        ref = piece_ref(j, core, piece)
        recv = (sib_recv if dev is sib else tok_recv).at[j * 4 + piece]
        copy = pltpu.make_async_remote_copy(
            src_ref=ref,
            dst_ref=ref,
            send_sem=tok_send.at[count[0]],
            recv_sem=recv,
            device_id=dev,
            device_id_type=MESH,
        )
        count[0] += 1
        sent.append(copy)
        return copy

    def arrive(j, piece):
        ref = piece_ref(j, core, piece)
        pltpu.make_async_remote_copy(
            src_ref=ref,
            dst_ref=ref,
            send_sem=tok_send.at[0],
            recv_sem=tok_recv.at[j * 4 + piece],
            device_id=sib,
            device_id_type=MESH,
        ).wait_recv()

    def arrive_sib(j, piece):
        ref = piece_ref(j, 1 - core, piece)
        pltpu.make_async_remote_copy(
            src_ref=ref,
            dst_ref=ref,
            send_sem=tok_send.at[0],
            recv_sem=sib_recv.at[j * 4 + piece],
            device_id=sib,
            device_id_type=MESH,
        ).wait_recv()

    send(j_own, 0, x_up).start()
    send(j_own, 2, x_dn).start()
    send(j_own, 0, y_up).start()
    send(j_own, 2, y_dn).start()
    norm(core, 1)
    norm(core, 3)
    send(j_own, 1, x_up).start()
    send(j_own, 3, x_dn).start()
    send(j_own, 1, y_up).start()
    send(j_own, 3, y_dn).start()
    send(j_own, 2, x_up).start()
    send(j_own, 0, x_dn).start()
    send(j_own, 3, x_up).start()
    send(j_own, 1, x_dn).start()

    CHUNK = 128
    last = nz // 2 - 1
    ways = (True, False)
    turns = [(c, k, up) for c in (1, 0) for k in range(3) for up in ways]

    def goes(step, up, c):
        return step < last or (step == last and c == (0 if up else 1))

    def z_copy(s, step, up, c, k):
        sems, recvs = (zp_send, zp_recv) if up else (zm_send, zm_recv)
        ref = slabs.at[c, s, pl.ds(k * CHUNK, CHUNK), :]
        return pltpu.make_async_remote_copy(
            src_ref=ref,
            dst_ref=ref,
            send_sem=sems.at[step * 6 + c * 3 + k],
            recv_sem=recvs.at[step * 6 + c * 3 + k],
            device_id=(z_up[0], y_hi * 2) if straight(step, up, c) else z_up if up else z_dn,
            device_id_type=MESH,
        )

    def straight(step, up, c):
        return step == last and up and c == 0

    def z_out(step, up, c, k):
        return z_copy((z + nz - step) % nz if up else (z + step) % nz, step, up, c, k)

    def z_in(step, up, c, k):
        return z_copy(z_slab(step, up), step, up, c, k)

    def z_slab(step, up):
        return (z + 2 * nz - step - 1) % nz if up else (z + step + 1) % nz

    def hand_over(s, n):
        ref = slabs.at[0, s]
        return pltpu.make_async_remote_copy(
            src_ref=ref,
            dst_ref=ref,
            send_sem=sl_send.at[n],
            recv_sem=sl_recv.at[n],
            device_id=sib,
            device_id_type=MESH,
        )

    def came(step):
        if step < 0:
            return [(z, 15)]
        if step == last:
            return [(z_slab(step, True), step * 2)]
        return [(z_slab(step, up), step * 2 + (0 if up else 1)) for up in ways]

    @pl.when(core == 1)
    def _():
        slabs[1, z, pl.ds(pl.multiple_of(q * 48, 16), 48), :] = wpack[q]
        for c in (1, 0):
            for d in range(c, GROUP):
                ref = w_rows(c, (q + 8 - d) % 8)
                pltpu.make_async_remote_copy(
                    src_ref=ref,
                    dst_ref=ref,
                    send_sem=wa_send.at[d],
                    recv_sem=wa_recv.at[c * 8 + d],
                    device_id=sib,
                    device_id_type=MESH,
                ).wait_recv()
            for k in range(3):
                z_out(0, True, c, k).start()
                z_out(0, False, c, k).start()
        hand_over(z, 15).start()

    def unpack(s, n):
        @pl.when(core == 0)
        def _():
            if n == 2 * last:
                for k in range(3):
                    z_in(last, True, 0, k).wait_recv()
            else:
                hand_over(s, n).wait_recv()

        at = pl.multiple_of(s * 256, 256)
        for g in range(GROUP):
            v = slabs[core, s, g * 48 + 32 : g * 48 + 48, :]
            wfull[pl.ds(at + g * 32, 32), 0:LANES] = slabs[core, s, g * 48 : g * 48 + 32, :]
            wfull[pl.ds(at + g * 32, 16), LANES:] = v
            wfull[pl.ds(at + g * 32 + 16, 16), LANES:] = swap(v.astype(F32)).astype(BF16)

    def unpacks(step):
        return [functools.partial(unpack, s, n) for s, n in came(step)]

    def z_round(step, tasks):
        @pl.when(core == 1)
        def _():
            todo = list(tasks)
            for c, k, up in turns:
                if goes(step, up, c) and not straight(step, up, c):
                    z_in(step, up, c, k).wait_recv()
                if goes(step + 1, up, c):
                    z_out(step + 1, up, c, k).start()
                if (c, k, up) == turns[-1] and step < last:
                    for s, n in came(step):
                        hand_over(s, n).start()
                if todo:
                    todo.pop(0)()
            for task in todo:
                task()

        @pl.when(core == 0)
        def _():
            for task in tasks:
                task()

    for copy in fetch[3:]:
        copy.wait()
    lanes_q = pl.ds(pl.multiple_of(tile * LANES, LANES), LANES)
    ones8 = jnp.ones((8, LANES), F32)
    subf = sub.astype(F32)

    def constants(first):
        dec = pick(dec_ref[:, lanes_q], left16)
        amp = pick(res_ref[:, lanes_q], left16) * jnp.sqrt(2.0 * dec)
        for s in (first, first + 1):
            d8 = dec[s : s + 1, :] * ones8
            amp_s[s] = amp[s : s + 1, :] * ones8
            lam_s[s] = jnp.exp(-d8)
            l62_s[s] = jnp.exp(-d8 * 62.0)
            l64_s[s] = jnp.exp(-d8 * 64.0)
            for i, sh in enumerate((1, 2, 4)):
                step_s[i, s] = jnp.where(sub >= sh, jnp.exp(-d8 * (128.0 * sh)), 0.0)
            pow_s[s] = jnp.exp(-d8 * (128.0 * subf))

    def z_weights():
        dec = pick(dec_ref[:, lanes_q], left16)
        dec_p = jnp.where(left, dec[0:8, :], dec[8:16, :])
        for s in range(nz):
            gap = (z - 1 - s).astype(F32)
            zw_s[s] = jnp.where(s < z, jnp.exp(-dec_p * (1024.0 * jnp.maximum(gap, 0.0))), 0.0)

    left64 = lax.broadcasted_iota(jnp.int32, (HALF, LANES), 1) < HALF

    def products(j, steps):
        acc = None
        for d in steps:
            at = pl.multiple_of(((z + nz + d) % nz) * 256, 256)
            term = jnp.dot(X[j, :, pl.ds(at, 256)], wfull[pl.ds(at, 256), :], preferred_element_type=F32)
            acc = term if acc is None else acc + term
        return acc

    def here(j):
        for piece in range(4):
            arrive_sib(j, piece)

    def add_products(j, steps, first):
        if first and j is not j_own:
            here(j)
        acc = products(j, steps)
        part[j] = acc if first else part[j] + acc

    def product_tasks(j, reach, each=3):
        steps = sorted(range(-reach, reach + 1), key=abs)
        return [
            functools.partial(add_products, j, steps[i : i + each], i == 0) for i in range(0, len(steps), each)
        ]

    def finish(j, acc):
        t0a, t0b = acc[0:HALF, 0:LANES], acc[HALF:, 0:LANES]
        t1a, t1b = acc[0:HALF, LANES:], acc[HALF:, LANES:]
        rows = half_rows(j)
        for i, v in enumerate(
            (
                jnp.where(left64, t0a, swap(t0b)),
                jnp.where(left64, swap(t0a), t0b),
                jnp.where(left64, t1a, swap(t1b)),
            )
        ):
            proj[i, rows, :] = v.astype(BF16).astype(F32)

    units = [
        [(j_dn, 0, (x_up, y_up)), (j_up, 2, (x_dn, y_dn)), (p_own, 0, ()), (p_own, 2, ())],
        [(j_dn, 1, (x_up, y_up)), (j_up, 3, (x_dn, y_dn)), (p_own, 1, ()), (p_own, 3, ())],
        [(j_dn, 2, (y_dn,)), (j_up, 0, (y_up,)), (p_dn, 0, ()), (p_up, 2, ())],
        [(j_dn, 3, (y_dn,)), (j_up, 1, (y_up,)), (p_dn, 1, (x_up,)), (p_up, 3, (x_dn,))],
        [(j_op, 0, (y_up,)), (j_op, 2, (y_dn,)), (p_up, 0, ()), (p_dn, 2, ())],
        [(j_op, 1, ()), (j_op, 3, ()), (p_up, 1, ()), (p_dn, 3, ())],
        [(p_op, 0, ()), (p_op, 2, ()), (p_op, 1, ()), (p_op, 3, ())],
    ]
    waiting = []

    def unit(u):
        for j, piece, onward in units[u]:
            arrive(j, piece)
            for dev in onward:
                send(j, piece, dev).start()
            waiting.append((j, piece))

    def to_sibling():
        tasks = [send(j, piece, sib).start for j, piece in waiting]
        waiting.clear()
        return tasks

    def more(reach, *blocks):
        return [functools.partial(add_products, j, [reach, -reach], False) for j in blocks]

    def consts(*firsts):
        return [functools.partial(constants, s) for s in firsts]

    for piece in range(4):
        norm(1 - core, piece)
    unit(0)
    z_round(0, to_sibling() + unpacks(-1) + consts(0, 2))
    unit(1)
    z_round(1, to_sibling() + unpacks(0) + consts(4, 6, 8))
    unit(2)
    z_round(2, to_sibling() + unpacks(1) + consts(10, 12, 14))
    unit(3)
    z_round(3, to_sibling() + unpacks(2) + [z_weights])
    unit(4)
    z_round(4, to_sibling() + unpacks(3) + product_tasks(j_own, 4))
    z_round(5, to_sibling() + unpacks(4) + more(5, j_own) + product_tasks(p_own, 5))
    unit(5)
    z_round(6, to_sibling() + unpacks(5) + more(6, j_own, p_own) + product_tasks(j_dn, 6) + product_tasks(j_up, 6))
    unit(6)
    for task in to_sibling():
        task()
    z_round(
        7,
        unpacks(6)
        + more(7, j_own, p_own, j_dn, j_up)
        + product_tasks(j_op, 7)
        + product_tasks(p_up, 7)
        + product_tasks(p_dn, 7)
        + product_tasks(p_op, 7),
    )
    for task in unpacks(7):
        task()
    finish(7, part[7] + products(7, (-8,)))

    rim_copy = pltpu.make_async_remote_copy(
        src_ref=proj.at[:, 504:512, :],
        dst_ref=rim,
        send_sem=rim_sem.at[0],
        recv_sem=rim_sem.at[1],
        device_id=z_up,
        device_id_type=MESH,
    )
    rim_copy.start()
    for j in range(7):
        finish(j, part[j] + products(j, (-8,)))

    def at_step(i, r):
        return proj[i, pl.ds(r, 8, stride=HALF), :]

    def before(i, back, edge):
        last = swap(at_step(i, HALF - back))
        shifted = jnp.where(sub == 0, edge, pltpu.roll(last, 1, 0))
        return jnp.where(left, shifted, last)

    taps = [[pick(taps_ref[k, i : i + 1, lanes_q] * ones8, left) for i in range(3)] for k in range(3)]
    skp = pick(skip_ref[:, lanes_q] * ones8, left)

    def featurize(now, one, two):
        return [taps[0][i] * now[i] + taps[1][i] * one[i] + taps[2][i] * two[i] for i in range(3)]

    def scan_one(r, carry):
        one, two, states = carry
        now = [at_step(i, r) for i in range(3)]
        feats = featurize(now, one, two)
        drive = feats[1] * feats[2]
        drive_s[r] = drive
        gate_s[r] = feats[0]
        states = [lam_s[s] * states[s] + drive for s in range(MODES)]
        return now, one, states

    start = (
        [before(i, 1, 0.0) for i in range(3)],
        [before(i, 2, 0.0) for i in range(3)],
        [jnp.zeros((8, LANES), F32)] * MODES,
    )
    ends = lax.fori_loop(0, HALF, scan_one, start, unroll=4)[2]

    rim_copy.wait_recv()

    def edge(i, back):
        return jnp.where(z == 0, 0.0, swap(rim[i, 8 - back : 9 - back, :] * ones8))

    one = [before(i, 1, edge(i, 1)) for i in range(3)]
    two = [before(i, 2, edge(i, 2)) for i in range(3)]
    now = [at_step(i, 0) for i in range(3)]
    changes = []
    for r in range(2):
        feats = featurize(now, one, two)
        drive = feats[1] * feats[2]
        changes.append(drive - drive_s[r])
        drive_s[r] = drive
        gate_s[r] = feats[0]
        two, one, now = one, now, [at_step(i, 1) for i in range(3)]

    for s in range(MODES):
        e = ends[s] + l62_s[s] * (lam_s[s] * changes[0] + changes[1])
        sw = swap(e)
        el = jnp.where(left, e, sw)
        er = jnp.where(left, sw, e)
        g = l64_s[s] * el + er
        for i, sh in enumerate((1, 2, 4)):
            g = g + step_s[i, s] * pltpu.roll(g, sh, 0)
        end_s[0, s] = jnp.where(sub >= 1, pltpu.roll(g, 1, 0), 0.0)
        end_s[1, s] = el
        end_s[2, s] = g
    low = jnp.concatenate([end_s[2, s, 7:8, :] for s in range(8)], axis=0)
    high = jnp.concatenate([end_s[2, s, 7:8, :] for s in range(8, 16)], axis=0)
    totals[z] = jnp.where(left, low, high)

    def st_copy(d):
        return pltpu.make_async_remote_copy(
            src_ref=totals.at[z],
            dst_ref=totals.at[z],
            send_sem=st_send.at[d],
            recv_sem=st_recv.at[d],
            device_id=(((z + d) % nz) * 8 + q, ch),
            device_id_type=MESH,
        )

    far_first = sorted(range(1, nz), key=lambda d: -min(d, nz - d))
    for d in far_first:

        @pl.when(z + d < nz)
        def _(d=d):
            st_copy(d).start()

    for copy in sent:
        copy.wait_send()
    rim_copy.wait_send()

    @pl.loop(1, GROUP)
    def _(d):
        wa_copy(d).wait_send()

    @pl.when(core == 0)
    def _():
        wa_copy(0).wait_send()

    @pl.when(core == 1)
    def _():
        for step in range(last + 1):
            for c, k, up in turns:
                if goes(step, up, c):
                    z_out(step, up, c, k).wait_send()
        for step in range(-1, last):
            for s, n in came(step):
                hand_over(s, n).wait_send()

    for d in range(1, nz):

        @pl.when(z >= d)
        def _(d=d):
            s = (z + nz - d) % nz
            pltpu.make_async_remote_copy(
                src_ref=totals.at[s],
                dst_ref=totals.at[s],
                send_sem=st_send.at[d],
                recv_sem=st_recv.at[d],
                device_id=sib,
                device_id_type=MESH,
            ).wait_recv()

    into = jnp.zeros((8, LANES), F32)
    for s in range(nz):
        into = into + zw_s[s] * totals[s]
    into_r = swap(into)
    into_lo = jnp.where(left, into, into_r)
    into_hi = jnp.where(left, into_r, into)

    states = []
    for s in range(MODES):
        zc = (into_lo if s < 8 else into_hi)[s % 8 : s % 8 + 1, :]
        c = end_s[0, s] + pow_s[s] * zc
        states.append(jnp.where(left, c, l64_s[s] * c + end_s[1, s]))

    def scan_two(r, states):
        drive = drive_s[r]
        states = [lam_s[s] * states[s] + drive for s in range(MODES)]
        terms = [amp_s[s] * states[s] for s in range(MODES)]
        while len(terms) > 1:
            terms = [a + b for a, b in zip(terms[::2], terms[1::2])]
        obuf[pl.ds(pl.multiple_of(r * 8, 8), 8), :] = gate_s[r] * (terms[0] + skp * drive)
        return states

    lax.fori_loop(0, HALF, scan_two, states, unroll=4)

    for j in range(GROUP):
        outbuf[j] = obuf[pl.ds(j, HALF, stride=8), :].astype(BF16)

    def out_copy(d):
        to = (q + d) % 8
        return pltpu.make_async_remote_copy(
            src_ref=outbuf.at[to],
            dst_ref=inbox.at[q],
            send_sem=out_send.at[d],
            recv_sem=out_recv.at[d],
            device_id=(base + to, ch),
            device_id_type=MESH,
        )

    for d in (6, 2, 7, 5, 3, 1, 4):
        out_copy(d).start()

    inbox[q] = outbuf[q]

    for d in range(1, nz):

        @pl.when(z + d < nz)
        def _(d=d):
            st_copy(d).wait_send()

    @pl.loop(1, GROUP)
    def _(d):
        ref = inbox.at[(q + 8 - d) % 8]
        pltpu.make_async_remote_copy(
            src_ref=ref,
            dst_ref=ref,
            send_sem=out_send.at[d],
            recv_sem=out_recv.at[d],
            device_id=sib,
            device_id_type=MESH,
        ).wait_recv()
        out_copy(d).wait_send()

    for g in range(GROUP // 2):
        a = inbox[2 * g].astype(F32)
        b = inbox[2 * g + 1].astype(F32)
        cols = slice(g * LANES, (g + 1) * LANES)
        o_ref[0:HALF, cols] = jnp.where(left64, a, swap(b)).astype(BF16)
        o_ref[HALF:, cols] = jnp.where(left64, swap(a), b).astype(BF16)


def local(tokens, norm_gain, in_proj, short_taps, decay, residue, skip):
    rows, width = tokens.shape
    channels = in_proj.shape[2]
    nz = lax.axis_size("ctx") // GROUP
    weights = jnp.transpose(in_proj, (1, 0, 2))
    vmem = pl.BlockSpec(memory_space=pltpu.VMEM)
    dma = pltpu.SemaphoreType.DMA
    const = pltpu.VMEM((MODES, 8, LANES), F32)
    return pl.pallas_call(
        functools.partial(kernel, nz),
        out_shape=jax.ShapeDtypeStruct((rows, channels), BF16),
        in_specs=[pl.BlockSpec(memory_space=pl.ANY)] * 7,
        out_specs=vmem,
        scratch_shapes=[
            pltpu.VMEM((rows, width), BF16),
            pltpu.VMEM((1, width), F32),
            pltpu.VMEM((3, 32, channels), BF16),
            pltpu.VMEM((3, 3, channels), F32),
            pltpu.VMEM((MODES, channels), F32),
            pltpu.VMEM((MODES, channels), F32),
            pltpu.VMEM((1, channels), F32),
            pltpu.VMEM((GROUP, ROWS, width), BF16),
            pltpu.VMEM((GROUP, 48, LANES), BF16),
            pltpu.VMEM((2, nz, 384, LANES), BF16),
            pltpu.VMEM((width, 2 * LANES), BF16),
            pltpu.VMEM((GROUP, ROWS, 2 * LANES), F32),
            pltpu.VMEM((3, GROUP * HALF, LANES), F32),
            pltpu.VMEM((3, 8, LANES), F32),
            pltpu.VMEM((HALF, 8, LANES), F32),
            pltpu.VMEM((HALF, 8, LANES), F32),
            const,
            const,
            const,
            const,
            pltpu.VMEM((3, MODES, 8, LANES), F32),
            const,
            pltpu.VMEM((nz, 8, LANES), F32),
            pltpu.VMEM((3, MODES, 8, LANES), F32),
            pltpu.VMEM((nz, 8, LANES), F32),
            pltpu.VMEM((GROUP * HALF, LANES), F32),
            pltpu.VMEM((GROUP, HALF, LANES), BF16),
            pltpu.VMEM((GROUP, HALF, LANES), BF16),
            dma((8,)),
            dma((8,)),
            dma((16,)),
            dma((64,)),
            dma((32,)),
            dma((32,)),
            dma((48,)),
            dma((48,)),
            dma((48,)),
            dma((48,)),
            dma((16,)),
            dma((16,)),
            dma((2,)),
            dma((16,)),
            dma((16,)),
            dma((8,)),
            dma((8,)),
        ],
        compiler_params=pltpu.CompilerParams(
            collective_id=0, has_side_effects=True, vmem_limit_bytes=56 * 1024 * 1024
        ),
        name="hyena",
    )(
        tokens,
        norm_gain.reshape(1, width),
        weights,
        short_taps,
        decay,
        residue,
        skip.reshape(1, channels),
    )


def solution(mesh):
    placed = (
        P("ctx", None),
        P(),
        P("ctx", None, "ch"),
        P(None, None, "ch"),
        P(None, "ch"),
        P(None, "ch"),
        P("ch"),
    )
    return jax.shard_map(
        local, mesh=mesh, in_specs=placed, out_specs=P("ctx", "ch"), check_vma=False
    )
```

```python
import functools

import jax
import jax.numpy as jnp
from jax import lax
from jax.experimental import pallas as pl
from jax.experimental.pallas import tpu as pltpu
from jax.sharding import PartitionSpec as P

MESH = pl.DeviceIdType.MESH
F32 = jnp.float32
BF16 = jnp.bfloat16

ROWS = 128
GROUP = 8
PIECE = 16
LANES = 128
HALF = 64
MODES = 16


def kernel(
    nz,
    tok_hbm,
    gain_hbm,
    w_hbm,
    taps_hbm,
    dec_hbm,
    res_hbm,
    skip_hbm,
    o_ref,
    tok_ref,
    gain_ref,
    w_ref,
    taps_ref,
    dec_ref,
    res_ref,
    skip_ref,
    X,
    wpack,
    slabs,
    wfull,
    part,
    proj,
    rim,
    drive_s,
    gate_s,
    lam_s,
    amp_s,
    l62_s,
    l64_s,
    step_s,
    pow_s,
    zw_s,
    end_s,
    totals,
    obuf,
    outbuf,
    inbox,
    in_sem,
    wa_send,
    wa_recv,
    tok_send,
    tok_recv,
    sib_recv,
    zp_send,
    zp_recv,
    zm_send,
    zm_recv,
    sl_send,
    sl_recv,
    rim_sem,
    st_send,
    st_recv,
    out_send,
    out_recv,
):
    ctx = lax.axis_index("ctx")
    ch = lax.axis_index("ch")
    z = ctx // 8
    q = ctx % 8
    y_lo = q // 4
    x = q % 4
    y_hi = ch // 2
    core = ch % 2
    par = q % 2
    tile = q // 2
    base = z * 8

    def plane(yl, xx):
        return yl * 4 + xx

    x_up = (base + plane(y_lo, (x + 1) % 4), ch)
    x_dn = (base + plane(y_lo, (x + 3) % 4), ch)
    y = y_hi * 2 + y_lo
    y_a = (y + 1) % 4
    y_b = (y + 3) % 4
    y_up = (base + plane(y_a % 2, x), (y_a // 2) * 2 + core)
    y_dn = (base + plane(y_b % 2, x), (y_b // 2) * 2 + core)
    sib = (ctx, y_hi * 2 + (1 - core))
    z_up = (((z + 1) % nz) * 8 + q, ch)
    z_dn = (((z + nz - 1) % nz) * 8 + q, ch)
    y_far = (base + plane(1 - y_lo, x), (1 - y_hi) * 2 + core)

    def half_rows(half):
        return pl.ds(pl.multiple_of(half * HALF, HALF), HALF)

    pairs = (
        (w_hbm, w_ref),
        (tok_hbm.at[half_rows(core), :], tok_ref.at[half_rows(core), :]),
        (gain_hbm, gain_ref),
        (tok_hbm.at[half_rows(1 - core), :], tok_ref.at[half_rows(1 - core), :]),
        (dec_hbm, dec_ref),
        (res_hbm, res_ref),
        (taps_hbm, taps_ref),
        (skip_hbm, skip_ref),
    )
    fetch = [pltpu.make_async_copy(a, b, in_sem.at[i]) for i, (a, b) in enumerate(pairs)]
    for copy in fetch:
        copy.start()

    totals[...] = jnp.zeros_like(totals)

    barrier = pltpu.get_barrier_semaphore()

    def greet(dev):
        pl.semaphore_signal(barrier, inc=1, device_id=dev, device_id_type=MESH)

    @pl.when(core == 1)
    def _():
        @pl.loop(1, GROUP)
        def _(d):
            greet((base + (q + d) % 8, ch))
            greet((base + (q + d) % 8, y_hi * 2))

        greet(z_up)
        greet(z_dn)
        greet(y_far)

    @pl.when(core == 0)
    def _():
        for dev in (x_up, x_dn, y_up, y_dn):
            greet(dev)

    greet(sib)

    lane = lax.broadcasted_iota(jnp.int32, (8, LANES), 1)
    left = lane < HALF
    sub = lax.broadcasted_iota(jnp.int32, (8, LANES), 0)

    def swap(v):
        return pltpu.roll(v, HALF, 1)

    def pick(v, lf):
        r = swap(v)
        even = jnp.where(lf, v, r)
        odd = jnp.where(lf, r, v)
        return jnp.where(par == 0, even, odd)

    j_own = plane(y_lo, x)
    j_up = plane(y_lo, (x + 1) % 4)
    j_dn = plane(y_lo, (x + 3) % 4)
    j_op = plane(y_lo, (x + 2) % 4)
    p_own = plane(1 - y_lo, x)
    p_up = plane(1 - y_lo, (x + 1) % 4)
    p_dn = plane(1 - y_lo, (x + 3) % 4)
    p_op = plane(1 - y_lo, (x + 2) % 4)

    def norm(half, piece):
        rows = pl.ds(pl.multiple_of(half * HALF + piece * PIECE, PIECE), PIECE)
        v = tok_ref[rows, :].astype(F32)
        ms = jnp.mean(v * v, axis=1, keepdims=True)
        X[j_own, rows, :] = (v * lax.rsqrt(ms + 1e-06) * gain_ref[...]).astype(BF16)

    fetch[0].wait()
    left32 = lax.broadcasted_iota(jnp.int32, (32, LANES), 1) < HALF
    left16 = lax.broadcasted_iota(jnp.int32, (16, LANES), 1) < HALF
    for t in range(GROUP // 2):
        f0, f1, f2 = [w_ref[i, :, t * LANES : (t + 1) * LANES].astype(F32) for i in range(3)]
        r0, r1, r2 = swap(f0), swap(f1), swap(f2)
        wpack[2 * t, 0:32, :] = jnp.where(left32, f0, r1).astype(BF16)
        wpack[2 * t, 32:48, :] = jnp.where(left16, f2[0:16], r2[16:32]).astype(BF16)
        wpack[2 * t + 1, 0:32, :] = jnp.where(left32, r0, f1).astype(BF16)
        wpack[2 * t + 1, 32:48, :] = jnp.where(left16, r2[0:16], f2[16:32]).astype(BF16)
    fetch[1].wait()
    fetch[2].wait()
    norm(core, 0)
    norm(core, 2)
    pl.semaphore_wait(barrier, 12 - core)

    sent = []

    def w_rows(c, chip):
        return slabs.at[c, z, pl.ds(pl.multiple_of(chip * 48, 16), 48), :]

    def wa_copy(d):
        to = (q + d) % 8
        return pltpu.make_async_remote_copy(
            src_ref=wpack.at[to],
            dst_ref=w_rows(core, q),
            send_sem=wa_send.at[d],
            recv_sem=wa_recv.at[core * 8 + d],
            device_id=(base + to, y_hi * 2 + 1),
            device_id_type=MESH,
        )

    @pl.loop(1, GROUP)
    def _(d):
        wa_copy(d).start()

    @pl.when(core == 0)
    def _():
        wa_copy(0).start()

    count = [0]

    def piece_ref(j, half, piece):
        return X.at[j, pl.ds(pl.multiple_of(half * HALF + piece * PIECE, PIECE), PIECE), :]

    def send(j, piece, dev):
        ref = piece_ref(j, core, piece)
        recv = (sib_recv if dev is sib else tok_recv).at[j * 4 + piece]
        copy = pltpu.make_async_remote_copy(
            src_ref=ref,
            dst_ref=ref,
            send_sem=tok_send.at[count[0]],
            recv_sem=recv,
            device_id=dev,
            device_id_type=MESH,
        )
        count[0] += 1
        sent.append(copy)
        return copy

    def arrive(j, piece):
        ref = piece_ref(j, core, piece)
        pltpu.make_async_remote_copy(
            src_ref=ref,
            dst_ref=ref,
            send_sem=tok_send.at[0],
            recv_sem=tok_recv.at[j * 4 + piece],
            device_id=sib,
            device_id_type=MESH,
        ).wait_recv()

    def arrive_sib(j, piece):
        ref = piece_ref(j, 1 - core, piece)
        pltpu.make_async_remote_copy(
            src_ref=ref,
            dst_ref=ref,
            send_sem=tok_send.at[0],
            recv_sem=sib_recv.at[j * 4 + piece],
            device_id=sib,
            device_id_type=MESH,
        ).wait_recv()

    send(j_own, 0, x_up).start()
    send(j_own, 2, x_dn).start()
    send(j_own, 0, y_up).start()
    send(j_own, 2, y_dn).start()
    norm(core, 1)
    norm(core, 3)
    send(j_own, 1, x_up).start()
    send(j_own, 3, x_dn).start()
    send(j_own, 1, y_up).start()
    send(j_own, 3, y_dn).start()
    send(j_own, 2, x_up).start()
    send(j_own, 0, x_dn).start()
    send(j_own, 3, x_up).start()
    send(j_own, 1, x_dn).start()

    CHUNK = 128
    last = nz // 2 - 1
    ways = (True, False)
    turns = [(c, k, up) for c in (1, 0) for k in range(3) for up in ways]

    def goes(step, up, c):
        return step < last or (step == last and c == (0 if up else 1))

    def z_copy(s, step, up, c, k):
        sems, recvs = (zp_send, zp_recv) if up else (zm_send, zm_recv)
        ref = slabs.at[c, s, pl.ds(k * CHUNK, CHUNK), :]
        return pltpu.make_async_remote_copy(
            src_ref=ref,
            dst_ref=ref,
            send_sem=sems.at[step * 6 + c * 3 + k],
            recv_sem=recvs.at[step * 6 + c * 3 + k],
            device_id=(z_up[0], y_hi * 2) if straight(step, up, c) else z_up if up else z_dn,
            device_id_type=MESH,
        )

    def straight(step, up, c):
        return step == last and up and c == 0

    def z_out(step, up, c, k):
        return z_copy((z + nz - step) % nz if up else (z + step) % nz, step, up, c, k)

    def z_in(step, up, c, k):
        return z_copy(z_slab(step, up), step, up, c, k)

    def z_slab(step, up):
        return (z + 2 * nz - step - 1) % nz if up else (z + step + 1) % nz

    def hand_over(s, n):
        ref = slabs.at[0, s]
        return pltpu.make_async_remote_copy(
            src_ref=ref,
            dst_ref=ref,
            send_sem=sl_send.at[n],
            recv_sem=sl_recv.at[n],
            device_id=sib,
            device_id_type=MESH,
        )

    def came(step):
        if step < 0:
            return [(z, 15)]
        if step == last:
            return [(z_slab(step, True), step * 2)]
        return [(z_slab(step, up), step * 2 + (0 if up else 1)) for up in ways]

    @pl.when(core == 1)
    def _():
        slabs[1, z, pl.ds(pl.multiple_of(q * 48, 16), 48), :] = wpack[q]
        for c in (1, 0):
            for d in range(c, GROUP):
                ref = w_rows(c, (q + 8 - d) % 8)
                pltpu.make_async_remote_copy(
                    src_ref=ref,
                    dst_ref=ref,
                    send_sem=wa_send.at[d],
                    recv_sem=wa_recv.at[c * 8 + d],
                    device_id=sib,
                    device_id_type=MESH,
                ).wait_recv()
            for k in range(3):
                z_out(0, True, c, k).start()
                z_out(0, False, c, k).start()
        hand_over(z, 15).start()

    def unpack(s, n):
        @pl.when(core == 0)
        def _():
            if n == 2 * last:
                for k in range(3):
                    z_in(last, True, 0, k).wait_recv()
            else:
                hand_over(s, n).wait_recv()

        at = pl.multiple_of(s * 256, 256)
        for g in range(GROUP):
            v = slabs[core, s, g * 48 + 32 : g * 48 + 48, :]
            wfull[pl.ds(at + g * 32, 32), 0:LANES] = slabs[core, s, g * 48 : g * 48 + 32, :]
            wfull[pl.ds(at + g * 32, 16), LANES:] = v
            wfull[pl.ds(at + g * 32 + 16, 16), LANES:] = swap(v.astype(F32)).astype(BF16)

    def unpacks(step):
        return [functools.partial(unpack, s, n) for s, n in came(step)]

    def z_round(step, tasks):
        @pl.when(core == 1)
        def _():
            todo = list(tasks)
            for c, k, up in turns:
                if goes(step, up, c) and not straight(step, up, c):
                    z_in(step, up, c, k).wait_recv()
                if goes(step + 1, up, c):
                    z_out(step + 1, up, c, k).start()
                if (c, k, up) == turns[-1] and step < last:
                    for s, n in came(step):
                        hand_over(s, n).start()
                if todo:
                    todo.pop(0)()
            for task in todo:
                task()

        @pl.when(core == 0)
        def _():
            for task in tasks:
                task()

    for copy in fetch[3:]:
        copy.wait()
    lanes_q = pl.ds(pl.multiple_of(tile * LANES, LANES), LANES)
    ones8 = jnp.ones((8, LANES), F32)
    subf = sub.astype(F32)

    def constants(first):
        dec = pick(dec_ref[:, lanes_q], left16)
        amp = pick(res_ref[:, lanes_q], left16) * jnp.sqrt(2.0 * dec)
        for s in (first, first + 1):
            d8 = dec[s : s + 1, :] * ones8
            amp_s[s] = amp[s : s + 1, :] * ones8
            lam_s[s] = jnp.exp(-d8)
            l62_s[s] = jnp.exp(-d8 * 62.0)
            l64_s[s] = jnp.exp(-d8 * 64.0)
            for i, sh in enumerate((1, 2, 4)):
                step_s[i, s] = jnp.where(sub >= sh, jnp.exp(-d8 * (128.0 * sh)), 0.0)
            pow_s[s] = jnp.exp(-d8 * (128.0 * subf))

    def z_weights():
        dec = pick(dec_ref[:, lanes_q], left16)
        dec_p = jnp.where(left, dec[0:8, :], dec[8:16, :])
        for s in range(nz):
            gap = (z - 1 - s).astype(F32)
            zw_s[s] = jnp.where(s < z, jnp.exp(-dec_p * (1024.0 * jnp.maximum(gap, 0.0))), 0.0)

    left64 = lax.broadcasted_iota(jnp.int32, (HALF, LANES), 1) < HALF

    def products(j, steps):
        acc = None
        for d in steps:
            at = pl.multiple_of(((z + nz + d) % nz) * 256, 256)
            term = jnp.dot(X[j, :, pl.ds(at, 256)], wfull[pl.ds(at, 256), :], preferred_element_type=F32)
            acc = term if acc is None else acc + term
        return acc

    def here(j):
        for piece in range(4):
            arrive_sib(j, piece)

    def add_products(j, steps, first):
        if first and j is not j_own:
            here(j)
        acc = products(j, steps)
        part[j] = acc if first else part[j] + acc

    def product_tasks(j, reach, each=3):
        steps = sorted(range(-reach, reach + 1), key=abs)
        return [
            functools.partial(add_products, j, steps[i : i + each], i == 0) for i in range(0, len(steps), each)
        ]

    def finish(j, acc):
        t0a, t0b = acc[0:HALF, 0:LANES], acc[HALF:, 0:LANES]
        t1a, t1b = acc[0:HALF, LANES:], acc[HALF:, LANES:]
        rows = half_rows(j)
        for i, v in enumerate(
            (
                jnp.where(left64, t0a, swap(t0b)),
                jnp.where(left64, swap(t0a), t0b),
                jnp.where(left64, t1a, swap(t1b)),
            )
        ):
            proj[i, rows, :] = v.astype(BF16).astype(F32)

    units = [
        [(j_dn, 0, (x_up, y_up)), (j_up, 2, (x_dn, y_dn)), (p_own, 0, ()), (p_own, 2, ())],
        [(j_dn, 1, (x_up, y_up)), (j_up, 3, (x_dn, y_dn)), (p_own, 1, ()), (p_own, 3, ())],
        [(j_dn, 2, (y_dn,)), (j_up, 0, (y_up,)), (p_dn, 0, ()), (p_up, 2, ())],
        [(j_dn, 3, (y_dn,)), (j_up, 1, (y_up,)), (p_dn, 1, (x_up,)), (p_up, 3, (x_dn,))],
        [(j_op, 0, (y_up,)), (j_op, 2, (y_dn,)), (p_up, 0, ()), (p_dn, 2, ())],
        [(j_op, 1, ()), (j_op, 3, ()), (p_up, 1, ()), (p_dn, 3, ())],
        [(p_op, 0, ()), (p_op, 2, ()), (p_op, 1, ()), (p_op, 3, ())],
    ]
    waiting = []

    def unit(u):
        for j, piece, onward in units[u]:
            arrive(j, piece)
            for dev in onward:
                send(j, piece, dev).start()
            waiting.append((j, piece))

    def to_sibling():
        tasks = [send(j, piece, sib).start for j, piece in waiting]
        waiting.clear()
        return tasks

    def more(reach, *blocks):
        return [functools.partial(add_products, j, [reach, -reach], False) for j in blocks]

    def consts(*firsts):
        return [functools.partial(constants, s) for s in firsts]

    for piece in range(4):
        norm(1 - core, piece)
    unit(0)
    z_round(0, to_sibling() + unpacks(-1) + consts(0, 2))
    unit(1)
    z_round(1, to_sibling() + unpacks(0) + consts(4, 6, 8))
    unit(2)
    z_round(2, to_sibling() + unpacks(1) + consts(10, 12, 14))
    unit(3)
    z_round(3, to_sibling() + unpacks(2) + [z_weights])
    unit(4)
    z_round(4, to_sibling() + unpacks(3) + product_tasks(j_own, 4))
    z_round(5, to_sibling() + unpacks(4) + more(5, j_own) + product_tasks(p_own, 5))
    unit(5)
    z_round(6, to_sibling() + unpacks(5) + more(6, j_own, p_own) + product_tasks(j_dn, 6) + product_tasks(j_up, 6))
    unit(6)
    for task in to_sibling():
        task()
    z_round(
        7,
        unpacks(6)
        + more(7, j_own, p_own, j_dn, j_up)
        + product_tasks(j_op, 7)
        + product_tasks(p_up, 7)
        + product_tasks(p_dn, 7)
        + product_tasks(p_op, 7),
    )
    for task in unpacks(7):
        task()
    finish(7, part[7] + products(7, (-8,)))

    rim_copy = pltpu.make_async_remote_copy(
        src_ref=proj.at[:, 504:512, :],
        dst_ref=rim,
        send_sem=rim_sem.at[0],
        recv_sem=rim_sem.at[1],
        device_id=z_up,
        device_id_type=MESH,
    )
    rim_copy.start()
    for j in range(7):
        finish(j, part[j] + products(j, (-8,)))

    def at_step(i, r):
        return proj[i, pl.ds(r, 8, stride=HALF), :]

    def before(i, back, edge):
        last = swap(at_step(i, HALF - back))
        shifted = jnp.where(sub == 0, edge, pltpu.roll(last, 1, 0))
        return jnp.where(left, shifted, last)

    taps = [[pick(taps_ref[k, i : i + 1, lanes_q] * ones8, left) for i in range(3)] for k in range(3)]
    skp = pick(skip_ref[:, lanes_q] * ones8, left)

    def featurize(now, one, two):
        return [taps[0][i] * now[i] + taps[1][i] * one[i] + taps[2][i] * two[i] for i in range(3)]

    def scan_one(r, carry):
        one, two, states = carry
        now = [at_step(i, r) for i in range(3)]
        feats = featurize(now, one, two)
        drive = feats[1] * feats[2]
        drive_s[r] = drive
        gate_s[r] = feats[0]
        states = [lam_s[s] * states[s] + drive for s in range(MODES)]
        return now, one, states

    start = (
        [before(i, 1, 0.0) for i in range(3)],
        [before(i, 2, 0.0) for i in range(3)],
        [jnp.zeros((8, LANES), F32)] * MODES,
    )
    ends = lax.fori_loop(0, HALF, scan_one, start, unroll=4)[2]

    rim_copy.wait_recv()

    def edge(i, back):
        return jnp.where(z == 0, 0.0, swap(rim[i, 8 - back : 9 - back, :] * ones8))

    one = [before(i, 1, edge(i, 1)) for i in range(3)]
    two = [before(i, 2, edge(i, 2)) for i in range(3)]
    now = [at_step(i, 0) for i in range(3)]
    changes = []
    for r in range(2):
        feats = featurize(now, one, two)
        drive = feats[1] * feats[2]
        changes.append(drive - drive_s[r])
        drive_s[r] = drive
        gate_s[r] = feats[0]
        two, one, now = one, now, [at_step(i, 1) for i in range(3)]

    for s in range(MODES):
        e = ends[s] + l62_s[s] * (lam_s[s] * changes[0] + changes[1])
        sw = swap(e)
        el = jnp.where(left, e, sw)
        er = jnp.where(left, sw, e)
        g = l64_s[s] * el + er
        for i, sh in enumerate((1, 2, 4)):
            g = g + step_s[i, s] * pltpu.roll(g, sh, 0)
        end_s[0, s] = jnp.where(sub >= 1, pltpu.roll(g, 1, 0), 0.0)
        end_s[1, s] = el
        end_s[2, s] = g
    low = jnp.concatenate([end_s[2, s, 7:8, :] for s in range(8)], axis=0)
    high = jnp.concatenate([end_s[2, s, 7:8, :] for s in range(8, 16)], axis=0)
    totals[z] = jnp.where(left, low, high)

    def st_copy(d):
        return pltpu.make_async_remote_copy(
            src_ref=totals.at[z],
            dst_ref=totals.at[z],
            send_sem=st_send.at[d],
            recv_sem=st_recv.at[d],
            device_id=(((z + d) % nz) * 8 + q, ch),
            device_id_type=MESH,
        )

    far_first = sorted(range(1, nz), key=lambda d: -min(d, nz - d))
    for d in far_first:

        @pl.when(z + d < nz)
        def _(d=d):
            st_copy(d).start()

    for copy in sent:
        copy.wait_send()
    rim_copy.wait_send()

    @pl.loop(1, GROUP)
    def _(d):
        wa_copy(d).wait_send()

    @pl.when(core == 0)
    def _():
        wa_copy(0).wait_send()

    @pl.when(core == 1)
    def _():
        for step in range(last + 1):
            for c, k, up in turns:
                if goes(step, up, c):
                    z_out(step, up, c, k).wait_send()
        for step in range(-1, last):
            for s, n in came(step):
                hand_over(s, n).wait_send()

    for d in range(1, nz):

        @pl.when(z >= d)
        def _(d=d):
            s = (z + nz - d) % nz
            pltpu.make_async_remote_copy(
                src_ref=totals.at[s],
                dst_ref=totals.at[s],
                send_sem=st_send.at[d],
                recv_sem=st_recv.at[d],
                device_id=sib,
                device_id_type=MESH,
            ).wait_recv()

    into = jnp.zeros((8, LANES), F32)
    for s in range(nz):
        into = into + zw_s[s] * totals[s]
    into_r = swap(into)
    into_lo = jnp.where(left, into, into_r)
    into_hi = jnp.where(left, into_r, into)

    states = []
    for s in range(MODES):
        zc = (into_lo if s < 8 else into_hi)[s % 8 : s % 8 + 1, :]
        c = end_s[0, s] + pow_s[s] * zc
        states.append(jnp.where(left, c, l64_s[s] * c + end_s[1, s]))

    def scan_two(r, states):
        drive = drive_s[r]
        states = [lam_s[s] * states[s] + drive for s in range(MODES)]
        terms = [amp_s[s] * states[s] for s in range(MODES)]
        while len(terms) > 1:
            terms = [a + b for a, b in zip(terms[::2], terms[1::2])]
        obuf[pl.ds(pl.multiple_of(r * 8, 8), 8), :] = gate_s[r] * (terms[0] + skp * drive)
        return states

    lax.fori_loop(0, HALF, scan_two, states, unroll=4)

    def out_copy(d):
        to = (q + d) % 8
        return pltpu.make_async_remote_copy(
            src_ref=outbuf.at[to],
            dst_ref=inbox.at[q],
            send_sem=out_send.at[d],
            recv_sem=out_recv.at[d],
            device_id=(base + to, ch),
            device_id_type=MESH,
        )

    for d in (6, 2, 7, 5, 3, 1, 4):
        to = (q + d) % 8
        outbuf[to] = obuf[pl.ds(to, HALF, stride=8), :].astype(BF16)
        out_copy(d).start()

    inbox[q] = obuf[pl.ds(q, HALF, stride=8), :].astype(BF16)

    for d in range(1, nz):

        @pl.when(z + d < nz)
        def _(d=d):
            st_copy(d).wait_send()

    @pl.loop(1, GROUP)
    def _(d):
        ref = inbox.at[(q + 8 - d) % 8]
        pltpu.make_async_remote_copy(
            src_ref=ref,
            dst_ref=ref,
            send_sem=out_send.at[d],
            recv_sem=out_recv.at[d],
            device_id=sib,
            device_id_type=MESH,
        ).wait_recv()
        out_copy(d).wait_send()

    for g in range(GROUP // 2):
        a = inbox[2 * g].astype(F32)
        b = inbox[2 * g + 1].astype(F32)
        cols = slice(g * LANES, (g + 1) * LANES)
        o_ref[0:HALF, cols] = jnp.where(left64, a, swap(b)).astype(BF16)
        o_ref[HALF:, cols] = jnp.where(left64, swap(a), b).astype(BF16)


def local(tokens, norm_gain, in_proj, short_taps, decay, residue, skip):
    rows, width = tokens.shape
    channels = in_proj.shape[2]
    nz = lax.axis_size("ctx") // GROUP
    weights = jnp.transpose(in_proj, (1, 0, 2))
    vmem = pl.BlockSpec(memory_space=pltpu.VMEM)
    dma = pltpu.SemaphoreType.DMA
    const = pltpu.VMEM((MODES, 8, LANES), F32)
    return pl.pallas_call(
        functools.partial(kernel, nz),
        out_shape=jax.ShapeDtypeStruct((rows, channels), BF16),
        in_specs=[pl.BlockSpec(memory_space=pl.ANY)] * 7,
        out_specs=vmem,
        scratch_shapes=[
            pltpu.VMEM((rows, width), BF16),
            pltpu.VMEM((1, width), F32),
            pltpu.VMEM((3, 32, channels), BF16),
            pltpu.VMEM((3, 3, channels), F32),
            pltpu.VMEM((MODES, channels), F32),
            pltpu.VMEM((MODES, channels), F32),
            pltpu.VMEM((1, channels), F32),
            pltpu.VMEM((GROUP, ROWS, width), BF16),
            pltpu.VMEM((GROUP, 48, LANES), BF16),
            pltpu.VMEM((2, nz, 384, LANES), BF16),
            pltpu.VMEM((width, 2 * LANES), BF16),
            pltpu.VMEM((GROUP, ROWS, 2 * LANES), F32),
            pltpu.VMEM((3, GROUP * HALF, LANES), F32),
            pltpu.VMEM((3, 8, LANES), F32),
            pltpu.VMEM((HALF, 8, LANES), F32),
            pltpu.VMEM((HALF, 8, LANES), F32),
            const,
            const,
            const,
            const,
            pltpu.VMEM((3, MODES, 8, LANES), F32),
            const,
            pltpu.VMEM((nz, 8, LANES), F32),
            pltpu.VMEM((3, MODES, 8, LANES), F32),
            pltpu.VMEM((nz, 8, LANES), F32),
            pltpu.VMEM((GROUP * HALF, LANES), F32),
            pltpu.VMEM((GROUP, HALF, LANES), BF16),
            pltpu.VMEM((GROUP, HALF, LANES), BF16),
            dma((8,)),
            dma((8,)),
            dma((16,)),
            dma((64,)),
            dma((32,)),
            dma((32,)),
            dma((48,)),
            dma((48,)),
            dma((48,)),
            dma((48,)),
            dma((16,)),
            dma((16,)),
            dma((2,)),
            dma((16,)),
            dma((16,)),
            dma((8,)),
            dma((8,)),
        ],
        compiler_params=pltpu.CompilerParams(
            collective_id=0, has_side_effects=True, vmem_limit_bytes=56 * 1024 * 1024
        ),
        name="hyena",
    )(
        tokens,
        norm_gain.reshape(1, width),
        weights,
        short_taps,
        decay,
        residue,
        skip.reshape(1, channels),
    )


def solution(mesh):
    placed = (
        P("ctx", None),
        P(),
        P("ctx", None, "ch"),
        P(None, None, "ch"),
        P(None, "ch"),
        P(None, "ch"),
        P("ch"),
    )
    return jax.shard_map(
        local, mesh=mesh, in_specs=placed, out_specs=P("ctx", "ch"), check_vma=False
    )
```
